512 devices in a mesh: clu: 128 (over z, y, core), sub: 4 (over x).
Axes of the slice: x: 4, y: 8, z: 8, core: 2. Of those that a mesh axis runs over, the one named last changes fastest.
Arguments:
- p_dir: bfloat16 [256, 256, 512], P('clu', None, 'sub'), may hold values from -200 to 200
- q_dir: bfloat16 [256, 256, 512], P('clu', None, 'sub'), may hold values from -200 to 200
- mass: float32 [256, 512], P('clu', 'sub'), may hold values from 0.5 to 2
- nearby_tile_blocks: bfloat16 [256, 16, 512, 512], P('clu', None, None, 'sub'), may hold values from -0.09375 to 0.09375
- near_ids: int32 [256, 16], P('clu'), may hold values from 0 to 255, as said below
- near_count: int32 [256], P('clu'), may hold values from 4 to 16, as said below
- col_basis: bfloat16 [256, 64, 512], P('clu', None, 'sub'), may hold values from -0.25 to 0.25
- row_basis: bfloat16 [256, 64, 512], P('clu', None, 'sub'), may hold values from -0.75 to 0.75
- col_transfer: bfloat16 [256, 64, 64], P('clu'), may hold values from -0.75 to 0.75
- row_transfer: bfloat16 [256, 64, 64], P('clu'), may hold values from -0.75 to 0.75
- couplings: bfloat16 [128, 8, 64, 64], P('clu', 'sub'), may hold values from -0.25 to 0.25
- far_ids: int32 [128, 8], P('clu', 'sub'), may hold values from 0 to 127, as said below
Outputs:
- v_next: float32 [256, 256, 512], P('clu', None, 'sub')
- w_next: float32 [256, 256, 512], P('clu', None, 'sub')
- delta: float32 [256], replicated
The draws below stay inside these ranges and needn't reach their ends.
Inputs may be any that keep to these rules, and one draw needn't show every extreme that they name: `near_ids`: cluster c is kept with parent c // 2. Every slot names a cluster whose parent is within 3 of the cluster's own parent; slot 0 is the cluster itself; slots at or after near_count are padding and still obey the reach. Some slot reaches exactly 3 parents away. `near_count`: some cluster fills all 16 slots. `far_ids`: every slot of parent P names a parent within 6 of P; some slot reaches exactly 6.
All inputs are finite; a program needn't handle non-finite values.
Results may differ from the reference program's by a relative error of at most 0.00045.
Values may be sent and summed in bfloat16 or wider, within the bound.
A program may use at most 64 MiB of HBM per device.

```python
import math
import jax
import jax.numpy as jnp
from jax import lax

LEAF_PANELS = 512
R = 64
CHILDREN_PER_DAD = 2
NEAR_SLOTS = 16
FAR = 8
NEAR_RADIUS = 3
FAR_REACH = 6
RHS = 256
LEAF_CLUSTERS = 256
NP = 128


def draw_p_dir(key, part):
    key = jax.random.fold_in(key, 1)
    primary_key, secondary_key = jax.random.split(key)
    ramp = (3.0 ** (jnp.arange(LEAF_CLUSTERS, dtype=jnp.float32) / max(LEAF_CLUSTERS - 1, 1)))[:, None, None]
    base = jax.random.normal(primary_key, (LEAF_CLUSTERS, RHS, LEAF_PANELS), jnp.float32)
    scale = jnp.exp(jax.random.uniform(secondary_key, (LEAF_CLUSTERS, RHS, 1), jnp.float32, -0.4, 0.4))
    return jnp.clip(base * scale * ramp, -200.0, 200.0).astype(jnp.bfloat16)


def draw_q_dir(key, part):
    key = jax.random.fold_in(key, 2)
    primary_key, secondary_key = jax.random.split(key)
    ramp = (3.0 ** (jnp.arange(LEAF_CLUSTERS, dtype=jnp.float32) / max(LEAF_CLUSTERS - 1, 1)))[:, None, None]
    base = jax.random.normal(primary_key, (LEAF_CLUSTERS, RHS, LEAF_PANELS), jnp.float32)
    scale = jnp.exp(jax.random.uniform(secondary_key, (LEAF_CLUSTERS, RHS, 1), jnp.float32, -0.4, 0.4))
    return jnp.clip(base * scale * ramp, -200.0, 200.0).astype(jnp.bfloat16)


def draw_near_ids(key, part):
    key = jax.random.fold_in(key, 3)
    primary_key, secondary_key = jax.random.split(key)
    parents = LEAF_CLUSTERS // CHILDREN_PER_DAD
    own = jnp.arange(LEAF_CLUSTERS, dtype=jnp.int32)[:, None] // CHILDREN_PER_DAD
    start_offset = jax.random.randint(primary_key, (LEAF_CLUSTERS, NEAR_SLOTS), -NEAR_RADIUS, NEAR_RADIUS + 1)
    member_index = jax.random.randint(secondary_key, (LEAF_CLUSTERS, NEAR_SLOTS), 0, CHILDREN_PER_DAD)
    target = own + start_offset
    target = jnp.where((target < 0) | (target >= parents), own - start_offset, target)
    chosen = (target * CHILDREN_PER_DAD + member_index).astype(jnp.int32)
    chosen = chosen.at[:, 0].set(jnp.arange(LEAF_CLUSTERS, dtype=jnp.int32))
    chosen = chosen.at[0, 1].set(NEAR_RADIUS * CHILDREN_PER_DAD)
    return chosen


def draw_near_count(key, part):
    key = jax.random.fold_in(key, 4)
    entry_counts = jax.random.randint(key, (LEAF_CLUSTERS,), NEAR_SLOTS // 4, NEAR_SLOTS + 1)
    entry_counts = entry_counts.at[0].set(NEAR_SLOTS)
    entry_counts = entry_counts.at[1].set(NEAR_SLOTS // 4)
    return entry_counts.astype(jnp.int32)


def draw_far_ids(key, part):
    key = jax.random.fold_in(key, 5)
    primary_key, secondary_key = jax.random.split(key)
    own = jnp.arange(NP, dtype=jnp.int32)[:, None]
    reach = jax.random.randint(primary_key, (NP, FAR), 1, FAR_REACH + 1)
    side = 2 * jax.random.randint(secondary_key, (NP, FAR), 0, 2) - 1
    target = jnp.clip(own + reach * side, 0, NP - 1)
    target = target.at[0, 0].set(FAR_REACH)
    return target.astype(jnp.int32)


def shard_levels(own_key, shape, cuts, smallest, largest):
    level, own = 1.0, jax.random.fold_in(own_key, 6)
    for dim, shards_of in cuts:
        draws = jnp.exp(jax.random.uniform(jax.random.fold_in(own, dim), (shards_of,), jnp.float32, smallest / len(cuts), largest / len(cuts)))
        level = level * jnp.repeat(draws, shape[dim] // shards_of).reshape([-1 if axis == dim else 1 for axis in range(len(shape))])
    return level


def gaussian(own_key, extent, deviation, bound, cuts=(), kind=jnp.bfloat16):
    result = deviation * jax.random.normal(own_key, extent, jnp.float32)
    if cuts:
        result = result * shard_levels(own_key, extent, cuts, -0.22, 0.18)
    return jnp.clip(result, -bound, bound).astype(kind)


def setup_inputs(seed: int = 0) -> dict:
    key_list = jax.random.split(jax.random.key(seed), 13)
    p_dir = draw_p_dir(jax.random.fold_in(key_list[12], 71), 0)
    q_dir = draw_q_dir(jax.random.fold_in(key_list[12], 71), 0)
    mass = jnp.clip(jnp.exp(math.log(2.0) - 1.3862944 * jax.random.uniform(key_list[2], (LEAF_CLUSTERS, LEAF_PANELS), jnp.float32) ** shard_levels(key_list[2], (LEAF_CLUSTERS, LEAF_PANELS), ((0, 128), (1, 4)), -0.2, 0.2)), 0.5, 2.0)
    nearby_tile_blocks = gaussian(key_list[3], (LEAF_CLUSTERS, NEAR_SLOTS, LEAF_PANELS, LEAF_PANELS), (LEAF_PANELS * NEAR_SLOTS // 2) ** -0.5, 0.09375, ((0, 128), (3, 4)))
    near_ids = draw_near_ids(jax.random.fold_in(key_list[12], 71), 0)
    near_count = draw_near_count(jax.random.fold_in(key_list[12], 71), 0)
    col_basis = gaussian(key_list[6], (LEAF_CLUSTERS, R, LEAF_PANELS), LEAF_PANELS ** -0.5, 0.25, ((0, 128), (2, 4)))
    row_basis = gaussian(key_list[7], (LEAF_CLUSTERS, R, LEAF_PANELS), R ** -0.5, 0.75, ((0, 128), (2, 4)))
    col_transfer = gaussian(key_list[8], (LEAF_CLUSTERS, R, R), R ** -0.5, 0.75, ((0, 128),))
    row_transfer = gaussian(key_list[9], (LEAF_CLUSTERS, R, R), R ** -0.5, 0.75, ((0, 128),))
    couplings = gaussian(key_list[10], (NP, FAR, R, R), (R * FAR) ** -0.5, 0.25, ((0, 128), (1, 4)))
    far_ids = draw_far_ids(jax.random.fold_in(key_list[12], 71), 0)
    return {"p_dir": p_dir, "q_dir": q_dir, "mass": mass, "nearby_tile_blocks": nearby_tile_blocks, "near_ids": near_ids, "near_count": near_count, "col_basis": col_basis, "row_basis": row_basis, "col_transfer": col_transfer, "row_transfer": row_transfer, "couplings": couplings, "far_ids": far_ids}


HIGH = lax.Precision.HIGHEST

def reference(p_dir, q_dir, mass, nearby_tile_blocks, near_ids, near_count, col_basis, row_basis, col_transfer, row_transfer, couplings, far_ids):
    f32 = jnp.float32
    p_full = p_dir.astype(f32)
    q_full = q_dir.astype(f32)
    pc = jnp.einsum('crn,ckn->crk', p_full, col_basis.astype(f32), precision=HIGH)
    qc = jnp.einsum('crn,ckn->crk', q_full, row_basis.astype(f32), precision=HIGH)
    pg = jnp.einsum('crk,ckl->crl', pc, col_transfer.astype(f32), precision=HIGH)
    pg = pg.reshape(NP, CHILDREN_PER_DAD, RHS, R).sum(axis=1)
    qg = jnp.einsum('crk,ckl->crl', qc, row_transfer.astype(f32), precision=HIGH)
    qg = qg.reshape(NP, CHILDREN_PER_DAD, RHS, R).sum(axis=1)
    coup = couplings.astype(f32)
    ph = jnp.einsum('psrl,pskl->prk', pg[far_ids], coup, precision=HIGH)
    terms = jnp.einsum('prk,pskl->psrl', qg, coup, precision=HIGH)
    qh = jnp.zeros((NP, RHS, R), f32).at[far_ids.reshape(-1)].add(terms.reshape(NP * FAR, RHS, R))
    parent_of = jnp.arange(LEAF_CLUSTERS) // CHILDREN_PER_DAD
    down_p = jnp.einsum('crl,ckl->crk', ph[parent_of], row_transfer.astype(f32), precision=HIGH)
    pf = jnp.einsum('crk,ckn->crn', down_p, row_basis.astype(f32), precision=HIGH)
    down_q = jnp.einsum('crl,ckl->crk', qh[parent_of], col_transfer.astype(f32), precision=HIGH)
    qf = jnp.einsum('crk,ckn->crn', down_q, col_basis.astype(f32), precision=HIGH)
    tile_slots = jnp.arange(NEAR_SLOTS)

    def near_step(acc, item):
        tiles, ids, count, q_row = item
        live = (tile_slots < count).astype(f32)
        tiles_full = tiles.astype(f32) * live[:, None, None]
        source = p_full[ids]
        out_a = jnp.einsum('smn,srn->rm', tiles_full, source, precision=HIGH)
        back = jnp.einsum('smn,rm->srn', tiles_full, q_row.astype(f32), precision=HIGH)
        return (acc.at[ids].add(back), out_a)
    qn, pn = lax.scan(near_step, jnp.zeros((LEAF_CLUSTERS, RHS, LEAF_PANELS), f32), (nearby_tile_blocks, near_ids, near_count, q_dir))
    half = 0.5 * mass[:, None, :]
    t_vec = half * p_full + pn + pf
    u_vec = half * q_full + qn + qf
    rho = jnp.sqrt(lax.optimization_barrier(jnp.sum(t_vec * t_vec, axis=(0, 2))) + 1e-06)
    xi_norm = jnp.sqrt(lax.optimization_barrier(jnp.sum(u_vec * u_vec, axis=(0, 2))) + 1e-06)
    v_next = t_vec / rho[None, :, None]
    w_next = u_vec / xi_norm[None, :, None]
    delta = lax.optimization_barrier(jnp.sum(v_next * w_next, axis=(0, 2)))
    return (v_next, w_next, delta)
```

```python
import functools

import jax
import jax.numpy as jnp
from jax import lax
from jax.experimental import pallas as pl
from jax.experimental.pallas import tpu as pltpu
from jax.sharding import PartitionSpec as P

NEAR = 3
FAR = 6
CORES = 2
CHIPS_Y = 8
MESH = pl.DeviceIdType.MESH
F32 = jnp.float32
BF16 = jnp.bfloat16
NEAR_SPAN = 2 * NEAR + 1
FAR_SPAN = 2 * FAR + 1


def mm(a, b):
    return lax.dot_general(a, b, (((1,), (0,)), ((), ())), preferred_element_type=F32)


def mm_nt(a, b):
    return lax.dot_general(a, b, (((1,), (1,)), ((), ())), preferred_element_type=F32)


def mm_tn(a, b):
    return lax.dot_general(a, b, (((0,), (0,)), ((), ())), preferred_element_type=F32)


def split(x):
    hi = x.astype(BF16)
    return hi, (x - hi.astype(F32)).astype(BF16)


def lane_half(shape):
    return lax.broadcasted_iota(jnp.int32, shape, 1) < shape[1] // 2


def kernel(
    sizes,
    table,
    p_ref,
    q_ref,
    mass_ref,
    col_ref,
    row_ref,
    colt_ref,
    rowt_ref,
    coup_ref,
    tiles_hbm,
    v_ref,
    w_ref,
    delta_ref,
    tiles,
    q_all,
    coup_all,
    p_win,
    up_part,
    up_recv,
    cw_hi,
    cw_lo,
    far_send,
    far_recv,
    chain,
    q_send,
    q_recv,
    pn_part,
    pn_recv,
    down_send,
    down_all,
    ar,
    tile_sem,
    q_ssem,
    q_rsem,
    c_ssem,
    c_rsem,
    p_ssem,
    p_rsem,
    up_ssem,
    up_rsem,
    far_ssem,
    far_rsem,
    qn_ssem,
    qn_rsem,
    pn_ssem,
    pn_rsem,
    down_ssem,
    down_rsem,
    ar_ssem,
    ar_rsem,
):
    n_clu, n_sub, n_y, slots = sizes
    n_z = n_clu // (n_y * CORES)
    clu = lax.axis_index("clu")
    sub = lax.axis_index("sub")
    core = lax.rem(clu, CORES)
    chip = clu // CORES
    y = lax.rem(chip, n_y)
    z = chip // n_y
    clusters, rhs, quarter = p_ref.shape
    block = rhs // n_sub

    def beside(offset):
        return (lax.rem(clu + (offset + n_clu), n_clu), sub)

    def peer(step):
        return lax.rem(sub + step, n_sub)

    groups = (
        (CORES * n_sub, sub * CORES + core, lambda i: (chip * CORES + lax.rem(i, CORES), i // CORES)),
        (n_y, y, lambda i: ((z * n_y + i) * CORES + core, sub)),
        (n_z, z, lambda i: ((i * n_y + y) * CORES + core, sub)),
    )

    def tile_copy(c):
        return pltpu.make_async_copy(tiles_hbm.at[c], tiles.at[c], tile_sem.at[c])

    for c in range(clusters):
        tile_copy(c).start()

    barrier = pltpu.get_barrier_semaphore()
    partners = 0
    for step in range(1, n_sub):
        pl.semaphore_signal(barrier, inc=1, device_id=(clu, peer(step)), device_id_type=MESH)
        partners += 1
    for offset in range(1, FAR + 1):
        for d in (-offset, offset):
            pl.semaphore_signal(barrier, inc=1, device_id=beside(d), device_id_type=MESH)
            partners += 1
    for size, mine, device in groups:
        for step in range(1, size):
            pl.semaphore_signal(barrier, inc=1, device_id=device(lax.rem(mine + step, size)), device_id_type=MESH)
            partners += 1

    q_all[sub] = q_ref[...]
    for j in range(coup_ref.shape[1]):
        own = coup_ref[0, j]
        coup_all[sub, j, :64] = jnp.concatenate([own, own], axis=1)
        coup_all[sub, j, 64:] = jnp.full((16, 128), table[78 + j].astype(F32), F32).astype(BF16)
    p_win[pl.ds(2 * NEAR, clusters)] = p_ref[...]
    p_win[2 * NEAR_SPAN] = jnp.zeros((rhs, quarter), BF16)
    chain[32] = jnp.zeros((rhs, quarter), F32)

    pl.semaphore_wait(barrier, partners)

    def to_peer(src, dst, ssem, rsem, step):
        return pltpu.make_async_remote_copy(
            src_ref=src, dst_ref=dst, send_sem=ssem, recv_sem=rsem, device_id=(clu, peer(step)), device_id_type=MESH
        )

    def to_side(src, dst, ssem, rsem, offset):
        return pltpu.make_async_remote_copy(
            src_ref=src, dst_ref=dst, send_sem=ssem, recv_sem=rsem, device_id=beside(offset), device_id_type=MESH
        )

    def q_copy(step):
        return to_peer(q_ref, q_all.at[sub], q_ssem.at[step - 1], q_rsem.at[step - 1], step)

    def c_copy(step):
        return to_peer(coup_all.at[sub], coup_all.at[sub], c_ssem.at[step - 1], c_rsem.at[step - 1], step)

    def up_copy(step):
        rows = pl.ds(pl.multiple_of(peer(step) * block, block), block)
        return to_peer(up_part.at[rows], up_recv.at[step - 1], up_ssem.at[step - 1], up_rsem.at[step - 1], step)

    def down_copy(step):
        return to_peer(down_send, down_all.at[sub], down_ssem.at[step - 1], down_rsem.at[step - 1], step)

    def pn_copy(step, c):
        return to_peer(
            pn_part.at[c, peer(step)],
            pn_recv.at[step - 1, c],
            pn_ssem.at[step - 1, c],
            pn_rsem.at[step - 1, c],
            step,
        )

    near_offsets = [d for k in range(NEAR, 0, -1) for d in (k, -k)]
    far_offsets = [d for k in range(FAR, 0, -1) for d in (k, -k)]

    def p_copy(i):
        d = near_offsets[i]
        there = (NEAR - d) * 2
        return to_side(p_ref, p_win.at[pl.ds(there, clusters)], p_ssem.at[i], p_rsem.at[i], d)

    def qn_copy(i):
        d = near_offsets[i]
        return to_side(q_send.at[i], q_recv.at[i], qn_ssem.at[i], qn_rsem.at[i], d)

    def far_copy(i):
        d = far_offsets[i]
        return to_side(far_send.at[i], far_recv.at[i], far_ssem.at[i], far_rsem.at[i], d)

    steps = range(1, n_sub)
    for step in steps:
        q_copy(step).start()
    for step in steps:
        c_copy(step).start()
    for i in range(len(near_offsets)):
        p_copy(i).start()

    up_hi, up_lo, down_hi, down_lo = [], [], [], []
    cols = [split(mm_tn(colt_ref[c], col_ref[c])) for c in range(clusters)]
    rows = [split(mm_tn(rowt_ref[c], row_ref[c])) for c in range(clusters)]
    none = jnp.zeros((cols[0][0].shape[0], clusters * quarter), BF16)
    col_hi, col_lo = (jnp.concatenate([x[k] for x in cols], axis=1) for k in range(2))
    row_hi, row_lo = (jnp.concatenate([x[k] for x in rows], axis=1) for k in range(2))

    def diagonal(a, b):
        return jnp.concatenate([jnp.concatenate([a, none], axis=1), jnp.concatenate([none, b], axis=1)], axis=0)

    both = jnp.concatenate([p_ref[0], p_ref[1], q_ref[0], q_ref[1]], axis=1)
    up_part[...] = mm_nt(both, diagonal(col_hi, row_hi)) + mm_nt(both, diagonal(col_lo, row_lo))
    for step in steps:
        up_copy(step).start()

    for step in steps:
        c_copy(step).wait()

    def gather_offset(w, carry):
        total = jnp.zeros((64, 128), F32)
        for s in range(n_sub):
            for j in range(coup_ref.shape[1]):
                here = coup_all[s, j, 64:65].astype(F32) == w.astype(F32)
                total = total + jnp.where(here, coup_all[s, j, :64].astype(F32), 0.0)
        hi, lo = split(total)
        cw_hi[w] = hi
        cw_lo[w] = lo
        return carry

    lax.fori_loop(0, FAR_SPAN, gather_offset, 0)

    for step in steps:
        up_copy(step).wait()
    up = up_part[pl.ds(pl.multiple_of(sub * block, block), block)]
    for step in steps:
        up = up + up_recv[step - 1]
    first = lane_half(up.shape)
    qg = up[:, 64:]
    qg_hi, qg_lo = split(qg)
    qg3 = jnp.concatenate([qg_hi, qg_lo, qg_hi], axis=1)

    def far_term(w):
        return mm(qg3, jnp.concatenate([cw_hi[w], cw_hi[w], cw_lo[w]], axis=0))

    for i, d in enumerate(far_offsets):
        far_send[i] = jnp.where(first, up, far_term(d + FAR))
        far_copy(i).start()
    own_far = jnp.where(first, up, far_term(FAR))

    for step in steps:
        q_copy(step).wait()
    for c in range(clusters):
        tile_copy(c).wait()
    for c in range(clusters):
        q_rows = jnp.concatenate([q_all[s, c] for s in range(n_sub)], axis=1)

        def back(k, carry, c=c, q_rows=q_rows):
            j = c * slots + 2 * k
            pair = jnp.concatenate([tiles[c, 2 * k], tiles[c, 2 * k + 1]], axis=1)
            out = mm(q_rows, pair)
            chain[j] = out[:, :quarter] + chain[table[j]]
            chain[j + 1] = out[:, quarter:] + chain[table[j + 1]]
            return carry

        lax.fori_loop(0, slots // 2, back, 0)
    for i, d in enumerate(near_offsets):
        for c in range(clusters):
            q_send[i, c] = chain[table[32 + 2 * (d + NEAR) + c]]
        qn_copy(i).start()

    for i in range(len(near_offsets)):
        p_copy(i).wait()
    for c in range(clusters):

        def front(k, carry, c=c):
            a = table[46 + c * slots + 2 * k]
            b = table[46 + c * slots + 2 * k + 1]
            source = jnp.concatenate([p_win[a], p_win[b]], axis=1)
            pair = jnp.concatenate([tiles[c, 2 * k], tiles[c, 2 * k + 1]], axis=1)
            out = mm_nt(source, pair)
            for s in range(n_sub):
                pn_part[c, s] += out[:, s * quarter : (s + 1) * quarter]
            return carry

        pn_part[c] = jnp.zeros_like(pn_part[c])
        lax.fori_loop(0, slots // 2, front, 0)
        for step in steps:
            pn_copy(step, c).start()

    def far_lhs(x):
        hi, lo = split(jnp.where(first, x, 0.0))
        return jnp.concatenate([hi, lo, hi], axis=1)

    def far_rhs(w):
        return jnp.concatenate([cw_hi[w], cw_hi[w], cw_lo[w]], axis=1)

    ph = mm_nt(far_lhs(own_far), far_rhs(FAR))
    total = own_far
    for i, d in enumerate(far_offsets):
        far_copy(i).wait()
        got = far_recv[i]
        ph = ph + mm_nt(far_lhs(got), far_rhs(FAR - d))
        total = total + got
    down_send[...] = jnp.where(first, jnp.concatenate([ph, ph], axis=1), total)
    for step in steps:
        down_copy(step).start()
    down_all[sub] = down_send[...]
    for step in steps:
        down_copy(step).wait()
    coeff = jnp.concatenate([down_all[s] for s in range(n_sub)], axis=0)
    coeff_hi, coeff_lo = split(coeff)
    coeff3 = jnp.concatenate([coeff_hi, coeff_lo, coeff_hi], axis=1)
    far_hi, far_lo = diagonal(row_hi, col_hi), diagonal(row_lo, col_lo)
    far_field = mm(coeff3, jnp.concatenate([far_hi, far_hi, far_lo], axis=0))

    for c in range(clusters):
        half = 0.5 * mass_ref[c : c + 1]
        v_ref[c] = half * p_ref[c].astype(F32) + far_field[:, c * quarter : (c + 1) * quarter]
        w_ref[c] = half * q_ref[c].astype(F32) + far_field[:, (clusters + c) * quarter : (clusters + c + 1) * quarter]

    for i in range(len(near_offsets)):
        qn_copy(i).wait()
    for c in range(clusters):
        u = w_ref[c] + chain[table[32 + 2 * NEAR + c]]
        for i in range(len(near_offsets)):
            u = u + q_recv[i, c]
        w_ref[c] = u
    for c in range(clusters):
        for step in steps:
            pn_copy(step, c).wait()
        t = v_ref[c] + pn_part[c, sub]
        for step in steps:
            t = t + pn_recv[step - 1, c]
        v_ref[c] = t

    def by_rhs(x):
        return jnp.sum(x.T, axis=0, keepdims=True)

    tt = by_rhs(v_ref[0] * v_ref[0] + v_ref[1] * v_ref[1])
    uu = by_rhs(w_ref[0] * w_ref[0] + w_ref[1] * w_ref[1])
    tu = by_rhs(v_ref[0] * w_ref[0] + v_ref[1] * w_ref[1])
    sums = jnp.concatenate([tt, uu, tu, jnp.zeros((5, rhs), F32)], axis=0)
    for g, (size, mine, device) in enumerate(groups):
        ar[g, mine] = sums

        def ar_copy(step, g=g, size=size, mine=mine, device=device):
            return pltpu.make_async_remote_copy(
                src_ref=ar.at[g, mine],
                dst_ref=ar.at[g, mine],
                send_sem=ar_ssem.at[g, step - 1],
                recv_sem=ar_rsem.at[g, step - 1],
                device_id=device(lax.rem(mine + step, size)),
                device_id_type=MESH,
            )

        for step in range(1, size):
            ar_copy(step).start()
        for step in range(1, size):
            ar_copy(step).wait()
        sums = ar[g, 0]
        for i in range(1, size):
            sums = sums + ar[g, i]

    rho = 1.0 / jnp.sqrt(sums[0:1] + 1e-06)
    xi = 1.0 / jnp.sqrt(sums[1:2] + 1e-06)
    delta_ref[...] = sums[2:3] * (rho * xi)
    rho_rows = jnp.broadcast_to(rho, (quarter, rhs)).T
    xi_rows = jnp.broadcast_to(xi, (quarter, rhs)).T
    for c in range(clusters):
        v_ref[c] = v_ref[c] * rho_rows
        w_ref[c] = w_ref[c] * xi_rows


def on_device(n_y, p_dir, q_dir, mass, tiles, near_ids, near_count, col, row, colt, rowt, coup, far_ids):
    clusters, rhs, quarter = p_dir.shape
    slots = tiles.shape[1]
    rank = col.shape[1]
    n_clu, n_sub = lax.axis_size("clu"), lax.axis_size("sub")
    block = rhs // n_sub
    here = lax.axis_index("clu")
    live = jnp.arange(slots, dtype=jnp.int32)[None, :] < near_count[:, None]
    local = near_ids - (here - NEAR) * clusters
    key = jnp.where(live, local, -1).reshape(-1)
    n_keys = clusters * slots
    wanted = jnp.concatenate([key, jnp.arange(clusters * NEAR_SPAN, dtype=jnp.int32)])
    limit = jnp.minimum(jnp.arange(wanted.shape[0], dtype=jnp.int32), n_keys)
    place = jnp.arange(n_keys, dtype=jnp.int32)
    same = (key[None, :] == wanted[:, None]) & (place[None, :] < limit[:, None])
    before = jnp.max(jnp.where(same, place[None, :], -1), axis=1)
    before = jnp.where(before < 0, n_keys, before)
    window = jnp.where(key < 0, clusters * NEAR_SPAN, key)
    table = jnp.concatenate([before, window, far_ids[0] - here + FAR])

    n_near, n_far = 2 * NEAR, 2 * FAR
    peers = n_sub - 1
    most = max(CORES * n_sub, n_y, n_clu // (n_y * CORES))
    vmem = pl.BlockSpec(memory_space=pltpu.VMEM)
    dma = pltpu.SemaphoreType.DMA
    v, w, delta = pl.pallas_call(
        functools.partial(kernel, (n_clu, n_sub, n_y, slots)),
        out_shape=(
            jax.ShapeDtypeStruct(p_dir.shape, F32),
            jax.ShapeDtypeStruct(p_dir.shape, F32),
            jax.ShapeDtypeStruct((1, rhs), F32),
        ),
        in_specs=[pl.BlockSpec(memory_space=pltpu.SMEM)] + [vmem] * 8 + [pl.BlockSpec(memory_space=pl.ANY)],
        out_specs=(vmem, vmem, vmem),
        scratch_shapes=[
            pltpu.VMEM(tiles.shape, BF16),
            pltpu.VMEM((n_sub, clusters, rhs, quarter), BF16),
            pltpu.VMEM((n_sub, coup.shape[1], rank + 16, 2 * rank), BF16),
            pltpu.VMEM((clusters * NEAR_SPAN + 1, rhs, quarter), BF16),
            pltpu.VMEM((rhs, 2 * rank), F32),
            pltpu.VMEM((peers, block, 2 * rank), F32),
            pltpu.VMEM((FAR_SPAN, rank, 2 * rank), BF16),
            pltpu.VMEM((FAR_SPAN, rank, 2 * rank), BF16),
            pltpu.VMEM((n_far, block, 2 * rank), F32),
            pltpu.VMEM((n_far, block, 2 * rank), F32),
            pltpu.VMEM((n_keys + 1, rhs, quarter), F32),
            pltpu.VMEM((n_near, clusters, rhs, quarter), F32),
            pltpu.VMEM((n_near, clusters, rhs, quarter), F32),
            pltpu.VMEM((clusters, n_sub, rhs, quarter), F32),
            pltpu.VMEM((peers, clusters, rhs, quarter), F32),
            pltpu.VMEM((block, 2 * rank), F32),
            pltpu.VMEM((n_sub, block, 2 * rank), F32),
            pltpu.VMEM((3, most, 8, rhs), F32),
            dma((clusters,)),
            dma((peers,)),
            dma((peers,)),
            dma((peers,)),
            dma((peers,)),
            dma((n_near,)),
            dma((n_near,)),
            dma((peers,)),
            dma((peers,)),
            dma((n_far,)),
            dma((n_far,)),
            dma((n_near,)),
            dma((n_near,)),
            dma((peers, clusters)),
            dma((peers, clusters)),
            dma((peers,)),
            dma((peers,)),
            dma((3, most)),
            dma((3, most)),
        ],
        compiler_params=pltpu.CompilerParams(
            collective_id=0, has_side_effects=True, vmem_limit_bytes=48 * 1024 * 1024
        ),
    )(table, p_dir, q_dir, mass, col, row, colt, rowt, coup, tiles)
    return v, w, delta.reshape(rhs)


def build(mesh, n_y):
    return jax.shard_map(
        functools.partial(on_device, n_y),
        mesh=mesh,
        in_specs=(
            P("clu", None, "sub"),
            P("clu", None, "sub"),
            P("clu", "sub"),
            P("clu", None, None, "sub"),
            P("clu", None),
            P("clu"),
            P("clu", None, "sub"),
            P("clu", None, "sub"),
            P("clu", None, None),
            P("clu", None, None),
            P("clu", "sub", None, None),
            P("clu", "sub"),
        ),
        out_specs=(P("clu", None, "sub"), P("clu", None, "sub"), P()),
        check_vma=False,
    )


def solution(mesh):
    return build(mesh, CHIPS_Y)
```

```python
import functools

import jax
import jax.numpy as jnp
from jax import lax
from jax.experimental import pallas as pl
from jax.experimental.pallas import tpu as pltpu
from jax.sharding import PartitionSpec as P

CORES = 2
CHIPS_Y = 8
NEAR_CHIPS = 2
FAR_CHIPS = 3
VMEM_BYTES = 64 * 1024 * 1024 - 64 * 1024
MESH = pl.DeviceIdType.MESH
F32 = jnp.float32
BF16 = jnp.bfloat16
NEAR_SPAN = CORES * (2 * NEAR_CHIPS + 1)
FAR_SPAN = CORES * (2 * FAR_CHIPS + 1)


def mm(a, b):
    return lax.dot_general(a, b, (((1,), (0,)), ((), ())), preferred_element_type=F32)


def mm_nt(a, b):
    return lax.dot_general(a, b, (((1,), (1,)), ((), ())), preferred_element_type=F32)


def mm_tn(a, b):
    return lax.dot_general(a, b, (((0,), (0,)), ((), ())), preferred_element_type=F32)


def split(x):
    hi = x.astype(BF16)
    return hi, (x - hi.astype(F32)).astype(BF16)


def lane_half(shape):
    return lax.broadcasted_iota(jnp.int32, shape, 1) < shape[1] // 2


def kernel(
    sizes,
    ids_ref,
    count_ref,
    far_ref,
    p_hbm,
    q_hbm,
    mass_hbm,
    col_hbm,
    row_hbm,
    colt_hbm,
    rowt_hbm,
    coup_hbm,
    tiles_hbm,
    t_hbm,
    u_hbm,
    scale_ref,
    table,
    t_ref,
    u_ref,
    mass_ref,
    col_ref,
    row_ref,
    colt_ref,
    rowt_ref,
    coup_ref,
    tiles,
    q_all,
    coup_all,
    p_win,
    up_part,
    up_recv,
    cw_hi,
    cw_lo,
    fx_send,
    fx_recv,
    far_send,
    far_recv,
    far_other,
    chain,
    ex_send,
    ex_recv,
    q_send,
    q_recv,
    pn_part,
    pn_recv,
    down_send,
    down_all,
    ar,
    out_sem,
    load_sem,
    tile_sem,
    q_ssem,
    q_rsem,
    c_ssem,
    c_rsem,
    p_ssem,
    p_rsem,
    up_ssem,
    up_rsem,
    fx_sem,
    far_ssem,
    far_rsem,
    ff_sem,
    ex_sem,
    qn_ssem,
    qn_rsem,
    pn_ssem,
    pn_rsem,
    down_ssem,
    down_rsem,
    ar_ssem,
    ar_rsem,
):
    n_clu, n_sub, n_y = sizes
    n_chips = n_clu // CORES
    n_z = n_chips // n_y
    clu = lax.axis_index("clu")
    sub = lax.axis_index("sub")
    core = lax.rem(clu, CORES)
    other = 1 - core
    chip = clu // CORES
    y = lax.rem(chip, n_y)
    z = chip // n_y
    toward = 2 * core - 1
    _, clusters, rhs, quarter = q_all.shape
    slots = tiles.shape[1]
    block = rhs // n_sub

    def on_chip(offset, which):
        return (lax.rem(chip + (offset + n_chips), n_chips) * CORES + which, sub)

    def peer(step):
        return lax.rem(sub + step, n_sub)

    sibling = (chip * CORES + other, sub)

    groups = (
        (CORES * n_sub, sub * CORES + core, lambda i: (chip * CORES + lax.rem(i, CORES), i // CORES)),
        (n_y, y, lambda i: ((z * n_y + i) * CORES + core, sub)),
        (n_z, z, lambda i: ((i * n_y + y) * CORES + core, sub)),
    )

    def near_parent(offset, which):
        return 2 * (NEAR_CHIPS + offset) + which

    def far_parent(offset, which):
        return 2 * (FAR_CHIPS + offset) + which

    def window(parent):
        return p_win.at[pl.ds(parent * clusters, clusters)]

    mine = near_parent(0, core)
    p_ref = window(mine)
    loads = [
        pltpu.make_async_copy(src, dst, load_sem.at[i])
        for i, (src, dst) in enumerate(
            (
                (p_hbm, p_ref),
                (q_hbm, q_all.at[sub]),
                (col_hbm, col_ref),
                (row_hbm, row_ref),
                (colt_hbm, colt_ref),
                (rowt_hbm, rowt_ref),
                (coup_hbm, coup_ref),
                (mass_hbm, mass_ref),
            )
        )
    ]

    def tile_copy(c):
        return pltpu.make_async_copy(tiles_hbm.at[c], tiles.at[c], tile_sem.at[c])

    barrier = pltpu.get_barrier_semaphore()
    partners = [device(lax.rem(place + step, size)) for size, place, device in groups for step in range(1, size)]
    partners += [on_chip(d, core) for k in range(1, FAR_CHIPS + 1) for d in (-k, k)]
    partners += [on_chip(2 * toward, other)]
    for partner in partners:
        pl.semaphore_signal(barrier, inc=1, device_id=partner, device_id_type=MESH)

    for load in loads:
        load.start()
    for c in range(clusters):
        tile_copy(c).start()

    n_keys = clusters * slots
    empty = p_win.shape[0] - 1
    at_last = n_keys
    at_block = n_keys + empty
    base = (chip - NEAR_CHIPS) * (CORES * clusters)
    for c in range(clusters):
        for s in range(slots):
            table[at_block + c * slots + s] = jnp.where(s < count_ref[c], ids_ref[c, s] - base, empty)

    def find(j, carry):
        wanted = table[at_block + j]
        found = jnp.int32(n_keys)
        for i in range(n_keys):
            found = jnp.where((table[at_block + i] == wanted) & (i < j), i, found)
        table[j] = found
        return carry

    def find_last(w, carry):
        found = jnp.int32(n_keys)
        for i in range(n_keys):
            found = jnp.where(table[at_block + i] == w, i, found)
        table[at_last + w] = found
        return carry

    p_win[empty] = jnp.zeros((rhs, quarter), BF16)
    chain[n_keys] = jnp.zeros((rhs, quarter), F32)
    for load in loads:
        load.wait()

    for j in range(coup_ref.shape[1]):
        coup_all[sub, j, :64] = coup_ref[0, j]
        far_place = far_ref[0, j] - (chip - FAR_CHIPS) * CORES
        coup_all[sub, j, 64:] = jnp.full((16, 64), far_place.astype(F32), F32).astype(BF16)

    cols = [split(mm_tn(colt_ref[c], col_ref[c])) for c in range(clusters)]
    rows = [split(mm_tn(rowt_ref[c], row_ref[c])) for c in range(clusters)]
    none = jnp.zeros((cols[0][0].shape[0], clusters * quarter), BF16)
    col_hi, col_lo = (jnp.concatenate([x[k] for x in cols], axis=1) for k in range(2))
    row_hi, row_lo = (jnp.concatenate([x[k] for x in rows], axis=1) for k in range(2))

    def diagonal(a, b):
        return jnp.concatenate([jnp.concatenate([a, none], axis=1), jnp.concatenate([none, b], axis=1)], axis=0)

    both = jnp.concatenate([p_ref[0], p_ref[1], q_all[sub, 0], q_all[sub, 1]], axis=1)
    up_part[...] = mm_nt(both, diagonal(col_hi, row_hi)) + mm_nt(both, diagonal(col_lo, row_lo))

    pl.semaphore_wait(barrier, len(partners))

    def remote(src, dst, ssem, rsem, device):
        return pltpu.make_async_remote_copy(
            src_ref=src, dst_ref=dst, send_sem=ssem, recv_sem=rsem, device_id=device, device_id_type=MESH
        )

    def to_peer(src, dst, ssem, rsem, step):
        return remote(src, dst, ssem, rsem, (clu, peer(step)))

    def q_copy(step):
        return to_peer(q_all.at[sub], q_all.at[sub], q_ssem.at[step - 1], q_rsem.at[step - 1], step)

    def c_copy(step):
        return to_peer(coup_all.at[sub], coup_all.at[sub], c_ssem.at[step - 1], c_rsem.at[step - 1], step)

    def up_copy(step):
        rows = pl.ds(pl.multiple_of(peer(step) * block, block), block)
        return to_peer(up_part.at[rows], up_recv.at[step - 1], up_ssem.at[step - 1], up_rsem.at[step - 1], step)

    def down_copy(step):
        return to_peer(down_send, down_all.at[sub], down_ssem.at[step - 1], down_rsem.at[step - 1], step)

    def pn_copy(step, c):
        return to_peer(
            pn_part.at[c, peer(step)],
            pn_recv.at[step - 1, c],
            pn_ssem.at[step - 1, c],
            pn_rsem.at[step - 1, c],
            step,
        )

    sides = (1, -1)

    def p_copy(i):
        if i < 2:
            source, there, device = mine, near_parent(-sides[i], core), on_chip(sides[i], core)
        elif i == 2:
            source, there, device = mine, near_parent(-2 * toward, core), on_chip(2 * toward, other)
        elif i == 3:
            source, there, device = mine, mine, sibling
        else:
            source = there = near_parent(-sides[i - 4], core)
            device = sibling
        return remote(window(source), window(there), p_ssem.at[i], p_rsem.at[i], device)

    far_sides = tuple(d for k in range(FAR_CHIPS, 0, -1) for d in (k, -k))

    def fx_copy():
        return remote(fx_send, fx_recv, fx_sem.at[0], fx_sem.at[1], sibling)

    def far_copy(i):
        return remote(far_send.at[i], far_recv.at[i], far_ssem.at[i], far_rsem.at[i], on_chip(far_sides[i], core))

    def ff_copy():
        return remote(far_recv, far_other, ff_sem.at[0], ff_sem.at[1], sibling)

    def ex_copy(e):
        return remote(ex_send.at[e + 1], ex_recv.at[e + 1], ex_sem.at[0, e + 1], ex_sem.at[1, e + 1], sibling)

    def qn_copy(i):
        device = on_chip(sides[i], core) if i < 2 else on_chip(2 * toward, other)
        return remote(q_send.at[i], q_recv.at[i], qn_ssem.at[i], qn_rsem.at[i], device)

    steps = range(1, n_sub)
    for step in steps:
        up_copy(step).start()
    for i in range(4):
        p_copy(i).start()
    for step in steps:
        c_copy(step).start()
    for step in steps:
        q_copy(step).start()

    lax.fori_loop(0, n_keys, find, 0)
    lax.fori_loop(0, empty, find_last, 0)

    for step in steps:
        c_copy(step).wait()

    def gather_offset(w, carry):
        total = jnp.zeros((64, 64), F32)
        for s in range(n_sub):
            for j in range(coup_ref.shape[1]):
                here = coup_all[s, j, 64:65].astype(F32) == w.astype(F32)
                total = total + jnp.where(here, coup_all[s, j, :64].astype(F32), 0.0)
        hi, lo = split(jnp.concatenate([total, total], axis=1))
        cw_hi[w] = hi
        cw_lo[w] = lo
        return carry

    lax.fori_loop(0, FAR_SPAN, gather_offset, 0)

    for step in steps:
        up_copy(step).wait()
    up = up_part[pl.ds(pl.multiple_of(sub * block, block), block)]
    for step in steps:
        up = up + up_recv[step - 1]
    first = lane_half(up.shape)
    qg_hi, qg_lo = split(up[:, 64:])
    qg3 = jnp.concatenate([qg_hi, qg_lo, qg_hi], axis=1)

    def far_term(w):
        return mm(qg3, jnp.concatenate([cw_hi[w], cw_hi[w], cw_lo[w]], axis=0))

    for e in range(-FAR_CHIPS, FAR_CHIPS + 1):
        fx_send[e + FAR_CHIPS] = far_term(far_parent(e, other))
    fx_copy().start()
    far_own = [far_term(far_parent(e, core)) for e in range(-FAR_CHIPS, FAR_CHIPS + 1)]
    far_recv[2 * FAR_CHIPS] = up
    fx_copy().wait()

    def far_tile(e):
        return jnp.where(first, up, far_own[e + FAR_CHIPS] + fx_recv[e + FAR_CHIPS])

    for i, e in enumerate(far_sides):
        far_send[i] = far_tile(e)
        far_copy(i).start()
    own_tile = far_tile(0)

    for i in range(2):
        p_copy(i).wait()
        p_copy(4 + i).start()

    for step in steps:
        q_copy(step).wait()
    for c in range(clusters):
        tile_copy(c).wait()
    for c in range(clusters):
        q_rows = jnp.concatenate([q_all[s, c] for s in range(n_sub)], axis=1)

        def back(k, carry, c=c, q_rows=q_rows):
            j = c * slots + 2 * k
            pair = jnp.concatenate([tiles[c, 2 * k], tiles[c, 2 * k + 1]], axis=1)
            out = mm(q_rows, pair)
            chain[j] = out[:, :quarter] + chain[table[j]]
            chain[j + 1] = out[:, quarter:] + chain[table[j + 1]]
            return carry

        lax.fori_loop(0, slots // 2, back, 0, unroll=slots // 2)

    def back_to(parent, c):
        return chain[table[at_last + clusters * parent + c]]

    for e in (1, -1, 0):
        for c in range(clusters):
            ex_send[e + 1, c] = back_to(near_parent(e, other), c)
        ex_copy(e).start()
    for c in range(clusters):
        q_send[2, c] = back_to(near_parent(2 * toward, other), c)
    qn_copy(2).start()

    for i in range(2, 6):
        p_copy(i).wait()

    def near_products(c):
        def front(k, carry):
            a = table[at_block + c * slots + 2 * k]
            b = table[at_block + c * slots + 2 * k + 1]
            source = jnp.concatenate([p_win[a], p_win[b]], axis=1)
            pair = jnp.concatenate([tiles[c, 2 * k], tiles[c, 2 * k + 1]], axis=1)
            out = mm_nt(source, pair)
            for s in range(n_sub):
                pn_part[c, s] += out[:, s * quarter : (s + 1) * quarter]
            return carry

        pn_part[c] = jnp.zeros_like(pn_part[c])
        lax.fori_loop(0, slots // 2, front, 0, unroll=slots // 2)
        for step in steps:
            pn_copy(step, c).start()

    near_products(0)
    for i, e in enumerate(sides):
        ex_copy(e).wait()
        for c in range(clusters):
            q_send[i, c] = back_to(near_parent(e, core), c) + ex_recv[e + 1, c]
        qn_copy(i).start()
    for c in range(1, clusters):
        near_products(c)

    def far_lhs(x):
        hi, lo = split(jnp.where(first, x, 0.0))
        return jnp.concatenate([hi, lo, hi], axis=1)

    def far_rhs(w):
        return jnp.concatenate([cw_hi[w], cw_hi[w], cw_lo[w]], axis=1)

    for i in range(len(far_sides)):
        far_copy(i).wait()
    ff_copy().start()
    ph = mm_nt(far_lhs(own_tile), far_rhs(far_parent(0, core)))
    total = own_tile
    for i, e in enumerate(far_sides):
        got = far_recv[i]
        ph = ph + mm_nt(far_lhs(got), far_rhs(far_parent(-e, core)))
        total = total + got
    ff_copy().wait()
    for i, e in enumerate(far_sides + (0,)):
        ph = ph + mm_nt(far_lhs(far_other[i]), far_rhs(far_parent(-e, other)))

    down_send[...] = jnp.where(first, jnp.concatenate([ph, ph], axis=1), total)
    for step in steps:
        down_copy(step).start()
    down_all[sub] = down_send[...]
    for step in steps:
        down_copy(step).wait()
    coeff = jnp.concatenate([down_all[s] for s in range(n_sub)], axis=0)
    coeff_hi, coeff_lo = split(coeff)
    coeff3 = jnp.concatenate([coeff_hi, coeff_lo, coeff_hi], axis=1)
    far_hi, far_lo = diagonal(row_hi, col_hi), diagonal(row_lo, col_lo)
    far_field = mm(coeff3, jnp.concatenate([far_hi, far_hi, far_lo], axis=0))

    ex_copy(0).wait()
    for c in range(clusters):
        half = 0.5 * mass_ref[c : c + 1]
        t_ref[c] = half * p_ref[c].astype(F32) + far_field[:, c * quarter : (c + 1) * quarter] + pn_part[c, sub]
        u = half * q_all[sub, c].astype(F32) + far_field[:, (clusters + c) * quarter : (clusters + c + 1) * quarter]
        u_ref[c] = u + (back_to(mine, c) + ex_recv[1, c])

    for c in range(clusters):
        for step in steps:
            pn_copy(step, c).wait()
        t = t_ref[c]
        for step in steps:
            t = t + pn_recv[step - 1, c]
        t_ref[c] = t
    for i in range(3):
        qn_copy(i).wait()
    for c in range(clusters):
        u_ref[c] = u_ref[c] + (q_recv[0, c] + q_recv[1, c] + q_recv[2, c])

    outs = [
        pltpu.make_async_copy(src, dst, out_sem.at[i]) for i, (src, dst) in enumerate(((t_ref, t_hbm), (u_ref, u_hbm)))
    ]
    for out in outs:
        out.start()

    def by_rhs(x):
        return jnp.sum(x.T, axis=0, keepdims=True)

    tt = by_rhs(t_ref[0] * t_ref[0] + t_ref[1] * t_ref[1])
    uu = by_rhs(u_ref[0] * u_ref[0] + u_ref[1] * u_ref[1])
    tu = by_rhs(t_ref[0] * u_ref[0] + t_ref[1] * u_ref[1])
    sums = jnp.concatenate([tt, uu, tu, jnp.zeros((5, rhs), F32)], axis=0)
    for g, (size, place, device) in enumerate(groups):
        ar[g, place] = sums

        def ar_copy(step, g=g, size=size, place=place, device=device):
            return pltpu.make_async_remote_copy(
                src_ref=ar.at[g, place],
                dst_ref=ar.at[g, place],
                send_sem=ar_ssem.at[g, step - 1],
                recv_sem=ar_rsem.at[g, step - 1],
                device_id=device(lax.rem(place + step, size)),
                device_id_type=MESH,
            )

        for step in range(1, size):
            ar_copy(step).start()
        for step in range(1, size):
            ar_copy(step).wait()
        sums = ar[g, 0]
        for i in range(1, size):
            sums = sums + ar[g, i]

    rho = 1.0 / jnp.sqrt(sums[0:1] + 1e-06)
    xi = 1.0 / jnp.sqrt(sums[1:2] + 1e-06)
    delta = sums[2:3] * (rho * xi)
    scale_ref[...] = jnp.concatenate([rho, xi, delta, jnp.zeros((5, rhs), F32)], axis=0)
    for out in outs:
        out.wait()


def scale_kernel(scale_ref, t_ref, u_ref, v_ref, w_ref, delta_ref):
    rhs, quarter = t_ref.shape[1:]
    v_ref[0] = t_ref[0] * jnp.broadcast_to(scale_ref[0:1], (quarter, rhs)).T
    w_ref[0] = u_ref[0] * jnp.broadcast_to(scale_ref[1:2], (quarter, rhs)).T
    delta_ref[...] = scale_ref[2:3]


def on_device(n_y, p_dir, q_dir, mass, tiles, near_ids, near_count, col, row, colt, rowt, coup, far_ids):
    clusters, rhs, quarter = p_dir.shape
    slots = tiles.shape[1]
    rank = col.shape[1]
    n_clu, n_sub = lax.axis_size("clu"), lax.axis_size("sub")
    block = rhs // n_sub
    n_keys = clusters * slots
    peers = n_sub - 1
    sides = 2 * FAR_CHIPS
    most = max(CORES * n_sub, n_y, n_clu // (n_y * CORES))
    vmem = pl.BlockSpec(memory_space=pltpu.VMEM)
    smem = pl.BlockSpec(memory_space=pltpu.SMEM)
    hbm = pl.BlockSpec(memory_space=pltpu.HBM)
    dma = pltpu.SemaphoreType.DMA
    whole = (clusters, rhs, quarter)
    t, u, scale = pl.pallas_call(
        functools.partial(kernel, (n_clu, n_sub, n_y)),
        out_shape=(
            jax.ShapeDtypeStruct(whole, F32),
            jax.ShapeDtypeStruct(whole, F32),
            jax.ShapeDtypeStruct((8, rhs), F32),
        ),
        in_specs=[smem] * 3 + [hbm] * 9,
        out_specs=(hbm, hbm, vmem),
        scratch_shapes=[
            pltpu.SMEM((2 * n_keys + clusters * NEAR_SPAN,), jnp.int32),
            pltpu.VMEM(whole, F32),
            pltpu.VMEM(whole, F32),
            pltpu.VMEM(mass.shape, F32),
            pltpu.VMEM(col.shape, BF16),
            pltpu.VMEM(col.shape, BF16),
            pltpu.VMEM(colt.shape, BF16),
            pltpu.VMEM(colt.shape, BF16),
            pltpu.VMEM(coup.shape, BF16),
            pltpu.VMEM(tiles.shape, BF16),
            pltpu.VMEM((n_sub, *whole), BF16),
            pltpu.VMEM((n_sub, coup.shape[1], rank + 16, rank), BF16),
            pltpu.VMEM((clusters * NEAR_SPAN + 1, rhs, quarter), BF16),
            pltpu.VMEM((rhs, 2 * rank), F32),
            pltpu.VMEM((peers, block, 2 * rank), F32),
            pltpu.VMEM((FAR_SPAN, rank, 2 * rank), BF16),
            pltpu.VMEM((FAR_SPAN, rank, 2 * rank), BF16),
            pltpu.VMEM((sides + 1, block, 2 * rank), F32),
            pltpu.VMEM((sides + 1, block, 2 * rank), F32),
            pltpu.VMEM((sides, block, 2 * rank), F32),
            pltpu.VMEM((sides + 1, block, 2 * rank), F32),
            pltpu.VMEM((sides + 1, block, 2 * rank), F32),
            pltpu.VMEM((n_keys + 1, rhs, quarter), F32),
            pltpu.VMEM((3, *whole), F32),
            pltpu.VMEM((3, *whole), F32),
            pltpu.VMEM((3, *whole), F32),
            pltpu.VMEM((3, *whole), F32),
            pltpu.VMEM((clusters, n_sub, rhs, quarter), F32),
            pltpu.VMEM((peers, *whole), F32),
            pltpu.VMEM((block, 2 * rank), F32),
            pltpu.VMEM((n_sub, block, 2 * rank), F32),
            pltpu.VMEM((3, most, 8, rhs), F32),
            dma((2,)),
            dma((8,)),
            dma((clusters,)),
            dma((peers,)),
            dma((peers,)),
            dma((peers,)),
            dma((peers,)),
            dma((6,)),
            dma((6,)),
            dma((peers,)),
            dma((peers,)),
            dma((2,)),
            dma((sides,)),
            dma((sides,)),
            dma((2,)),
            dma((2, 3)),
            dma((3,)),
            dma((3,)),
            dma((peers, clusters)),
            dma((peers, clusters)),
            dma((peers,)),
            dma((peers,)),
            dma((3, most)),
            dma((3, most)),
        ],
        compiler_params=pltpu.CompilerParams(
            collective_id=0, has_side_effects=True, vmem_limit_bytes=VMEM_BYTES
        ),
    )(near_ids, near_count, far_ids, p_dir, q_dir, mass, col, row, colt, rowt, coup, tiles)
    one = pl.BlockSpec((1, rhs, quarter), lambda c: (c, 0, 0))
    v, w, delta = pl.pallas_call(
        scale_kernel,
        grid=(clusters,),
        out_shape=(
            jax.ShapeDtypeStruct(whole, F32),
            jax.ShapeDtypeStruct(whole, F32),
            jax.ShapeDtypeStruct((1, rhs), F32),
        ),
        in_specs=[pl.BlockSpec((8, rhs), lambda c: (0, 0)), one, one],
        out_specs=(one, one, pl.BlockSpec((1, rhs), lambda c: (0, 0))),
        compiler_params=pltpu.CompilerParams(vmem_limit_bytes=VMEM_BYTES),
    )(scale, t, u)
    return v, w, delta.reshape(rhs)


def build(mesh, n_y):
    return jax.shard_map(
        functools.partial(on_device, n_y),
        mesh=mesh,
        in_specs=(
            P("clu", None, "sub"),
            P("clu", None, "sub"),
            P("clu", "sub"),
            P("clu", None, None, "sub"),
            P("clu", None),
            P("clu"),
            P("clu", None, "sub"),
            P("clu", None, "sub"),
            P("clu", None, None),
            P("clu", None, None),
            P("clu", "sub", None, None),
            P("clu", "sub"),
        ),
        out_specs=(P("clu", None, "sub"), P("clu", None, "sub"), P()),
        check_vma=False,
    )


def solution(mesh):
    return build(mesh, CHIPS_Y)
```

```python
import functools

import jax
import jax.numpy as jnp
from jax import lax
from jax.experimental import pallas as pl
from jax.experimental.pallas import tpu as pltpu
from jax.sharding import PartitionSpec as P

CORES = 2
CHIPS_Y = 8
NEAR_CHIPS = 2
FAR_CHIPS = 3
VMEM_BYTES = 64 * 1024 * 1024 - 64 * 1024
MESH = pl.DeviceIdType.MESH
F32 = jnp.float32
BF16 = jnp.bfloat16
NEAR_SPAN = CORES * (2 * NEAR_CHIPS + 1)
FAR_SPAN = CORES * (2 * FAR_CHIPS + 1)


def mm(a, b):
    return lax.dot_general(a, b, (((1,), (0,)), ((), ())), preferred_element_type=F32)


def mm_nt(a, b):
    return lax.dot_general(a, b, (((1,), (1,)), ((), ())), preferred_element_type=F32)


def mm_tn(a, b):
    return lax.dot_general(a, b, (((0,), (0,)), ((), ())), preferred_element_type=F32)


def split(x):
    hi = x.astype(BF16)
    return hi, (x - hi.astype(F32)).astype(BF16)


def lane_half(shape):
    return lax.broadcasted_iota(jnp.int32, shape, 1) < shape[1] // 2


def kernel(
    sizes,
    ids_ref,
    count_ref,
    far_ref,
    p_hbm,
    q_hbm,
    mass_hbm,
    col_hbm,
    row_hbm,
    colt_hbm,
    rowt_hbm,
    coup_hbm,
    tiles_hbm,
    t_hbm,
    u_hbm,
    scale_ref,
    table,
    t_ref,
    u_ref,
    mass_ref,
    col_ref,
    row_ref,
    colt_ref,
    rowt_ref,
    coup_ref,
    tiles,
    q_all,
    coup_all,
    p_win,
    up_part,
    up_recv,
    cw_hi,
    cw_lo,
    fx_send,
    fx_recv,
    far_send,
    far_recv,
    far_other,
    chain,
    ex_send,
    ex_recv,
    q_send,
    q_recv,
    pn_part,
    pn_mid,
    pn_recv,
    down_send,
    down_all,
    ar,
    out_sem,
    load_sem,
    tile_sem,
    q_ssem,
    q_rsem,
    c_ssem,
    c_rsem,
    p_ssem,
    p_rsem,
    up_ssem,
    up_rsem,
    fx_sem,
    far_ssem,
    far_rsem,
    ff_sem,
    ex_sem,
    qn_ssem,
    qn_rsem,
    mid_sem,
    pn_ssem,
    pn_rsem,
    down_ssem,
    down_rsem,
    ar_ssem,
    ar_rsem,
):
    n_clu, n_sub, n_y = sizes
    n_chips = n_clu // CORES
    n_z = n_chips // n_y
    clu = lax.axis_index("clu")
    sub = lax.axis_index("sub")
    core = lax.rem(clu, CORES)
    other = 1 - core
    chip = clu // CORES
    y = lax.rem(chip, n_y)
    z = chip // n_y
    toward = 2 * core - 1
    _, clusters, rhs, quarter = q_all.shape
    slots = tiles.shape[1]
    block = rhs // n_sub

    def on_chip(offset, which):
        return (lax.rem(chip + (offset + n_chips), n_chips) * CORES + which, sub)

    def peer(step):
        return lax.rem(sub + step, n_sub)

    sibling = (chip * CORES + other, sub)

    groups = (
        (CORES * n_sub, sub * CORES + core, lambda i: (chip * CORES + lax.rem(i, CORES), i // CORES)),
        (n_y, y, lambda i: ((z * n_y + i) * CORES + core, sub)),
        (n_z, z, lambda i: ((i * n_y + y) * CORES + core, sub)),
    )

    def near_parent(offset, which):
        return 2 * (NEAR_CHIPS + offset) + which

    def far_parent(offset, which):
        return 2 * (FAR_CHIPS + offset) + which

    def window(parent):
        return p_win.at[pl.ds(parent * clusters, clusters)]

    mine = near_parent(0, core)
    p_ref = window(mine)
    loads = [
        pltpu.make_async_copy(src, dst, load_sem.at[i])
        for i, (src, dst) in enumerate(
            (
                (p_hbm, p_ref),
                (q_hbm, q_all.at[sub]),
                (col_hbm, col_ref),
                (row_hbm, row_ref),
                (colt_hbm, colt_ref),
                (rowt_hbm, rowt_ref),
                (coup_hbm, coup_ref),
                (mass_hbm, mass_ref),
            )
        )
    ]

    def tile_copy(c):
        return pltpu.make_async_copy(tiles_hbm.at[c], tiles.at[c], tile_sem.at[c])

    barrier = pltpu.get_barrier_semaphore()
    partners = [device(lax.rem(place + step, size)) for size, place, device in groups for step in range(1, size)]
    partners += [on_chip(d, core) for k in range(1, FAR_CHIPS + 1) for d in (-k, k)]
    partners += [on_chip(d * toward, other) for d in (1, 2)]
    for partner in partners:
        pl.semaphore_signal(barrier, inc=1, device_id=partner, device_id_type=MESH)

    for load in loads:
        load.start()
    for c in range(clusters):
        tile_copy(c).start()

    n_keys = clusters * slots
    empty = p_win.shape[0] - 1
    at_last = n_keys
    at_block = n_keys + empty
    base = (chip - NEAR_CHIPS) * (CORES * clusters)
    for c in range(clusters):
        for s in range(slots):
            table[at_block + c * slots + s] = jnp.where(s < count_ref[c], ids_ref[c, s] - base, empty)

    def find(j, carry):
        wanted = table[at_block + j]
        found = jnp.int32(n_keys)
        for i in range(n_keys):
            found = jnp.where((table[at_block + i] == wanted) & (i < j), i, found)
        table[j] = found
        return carry

    def find_last(w, carry):
        found = jnp.int32(n_keys)
        for i in range(n_keys):
            found = jnp.where(table[at_block + i] == w, i, found)
        table[at_last + w] = found
        return carry

    p_win[empty] = jnp.zeros((rhs, quarter), BF16)
    chain[n_keys] = jnp.zeros((rhs, quarter), F32)
    for load in loads:
        load.wait()

    rank = coup_ref.shape[2]
    far_base = (chip - FAR_CHIPS) * CORES
    coup_all[sub, :rank] = jnp.concatenate([coup_ref[0, 0], coup_ref[0, 1]], axis=1)
    places = jnp.where(lane_half((16, 2 * rank)), far_ref[0, 0] - far_base, far_ref[0, 1] - far_base)
    coup_all[sub, rank:] = places.astype(F32).astype(BF16)

    cols = [split(mm_tn(colt_ref[c], col_ref[c])) for c in range(clusters)]
    rows = [split(mm_tn(rowt_ref[c], row_ref[c])) for c in range(clusters)]
    none = jnp.zeros((cols[0][0].shape[0], clusters * quarter), BF16)
    col_hi, col_lo = (jnp.concatenate([x[k] for x in cols], axis=1) for k in range(2))
    row_hi, row_lo = (jnp.concatenate([x[k] for x in rows], axis=1) for k in range(2))

    def diagonal(a, b):
        return jnp.concatenate([jnp.concatenate([a, none], axis=1), jnp.concatenate([none, b], axis=1)], axis=0)

    both = jnp.concatenate([p_ref[0], p_ref[1], q_all[sub, 0], q_all[sub, 1]], axis=1)
    up_part[...] = mm_nt(both, diagonal(col_hi, row_hi)) + mm_nt(both, diagonal(col_lo, row_lo))

    pl.semaphore_wait(barrier, len(partners))

    def remote(src, dst, ssem, rsem, device):
        return pltpu.make_async_remote_copy(
            src_ref=src, dst_ref=dst, send_sem=ssem, recv_sem=rsem, device_id=device, device_id_type=MESH
        )

    def to_peer(src, dst, ssem, rsem, step):
        return remote(src, dst, ssem, rsem, (clu, peer(step)))

    def q_copy(step):
        return to_peer(q_all.at[sub], q_all.at[sub], q_ssem.at[step - 1], q_rsem.at[step - 1], step)

    def c_copy(step):
        return to_peer(coup_all.at[sub], coup_all.at[sub], c_ssem.at[step - 1], c_rsem.at[step - 1], step)

    def up_copy(step):
        rows = pl.ds(pl.multiple_of(peer(step) * block, block), block)
        return to_peer(up_part.at[rows], up_recv.at[step - 1], up_ssem.at[step - 1], up_rsem.at[step - 1], step)

    def down_copy(step):
        return to_peer(down_send, down_all.at[sub], down_ssem.at[step - 1], down_rsem.at[step - 1], step)

    ways = (1, n_sub - 1)

    def mid_copy(c):
        return to_peer(pn_part.at[c, peer(2)], pn_mid.at[c], mid_sem.at[0, c], mid_sem.at[1, c], ways[c])

    def pn_copy(way, c):
        return to_peer(
            pn_part.at[c, peer(ways[way])], pn_recv.at[way, c], pn_ssem.at[way, c], pn_rsem.at[way, c], ways[way]
        )

    sides = (1, -1)

    def p_copy(i):
        if i < 2:
            source, there, device = mine, near_parent(-sides[i], core), on_chip(sides[i], core)
        elif i == 2:
            source, there, device = mine, near_parent(-2 * toward, core), on_chip(2 * toward, other)
        elif i == 3:
            source, there, device = mine, mine, sibling
        else:
            source = there = near_parent(-sides[i - 4], core)
            device = sibling
        return remote(window(source), window(there), p_ssem.at[i], p_rsem.at[i], device)

    far_sides = tuple(d for k in range(FAR_CHIPS, 0, -1) for d in (k, -k))

    def fx_copy():
        return remote(fx_send, fx_recv, fx_sem.at[0], fx_sem.at[1], sibling)

    def far_copy(i):
        return remote(far_send.at[i], far_recv.at[i], far_ssem.at[i], far_rsem.at[i], on_chip(far_sides[i], core))

    def ff_copy():
        return remote(far_recv, far_other, ff_sem.at[0], ff_sem.at[1], sibling)

    def ex_copy(i):
        return remote(ex_send.at[i], ex_recv.at[i], ex_sem.at[0, i], ex_sem.at[1, i], sibling)

    def qn_copy(i):
        device = (on_chip(toward, core), on_chip(-toward, core), on_chip(toward, other))[i]
        return remote(q_send.at[i], q_recv.at[i], qn_ssem.at[i], qn_rsem.at[i], device)

    steps = range(1, n_sub)
    for step in steps:
        up_copy(step).start()
    for i in range(4):
        p_copy(i).start()
    for step in steps:
        c_copy(step).start()
    for step in steps:
        q_copy(step).start()

    lax.fori_loop(0, n_keys, find, 0)
    lax.fori_loop(0, empty, find_last, 0)

    for step in steps:
        c_copy(step).wait()

    def gather_offset(w, carry):
        total = jnp.zeros((rank, 2 * rank), F32)
        for s in range(n_sub):
            here = coup_all[s, rank : rank + 1].astype(F32) == w.astype(F32)
            total = total + jnp.where(here, coup_all[s, :rank].astype(F32), 0.0)
        hi, lo = split(total + jnp.concatenate([total[:, rank:], total[:, :rank]], axis=1))
        cw_hi[w] = hi
        cw_lo[w] = lo
        return carry

    lax.fori_loop(0, FAR_SPAN, gather_offset, 0)

    for step in steps:
        up_copy(step).wait()
    up = up_part[pl.ds(pl.multiple_of(sub * block, block), block)]
    for step in steps:
        up = up + up_recv[step - 1]
    first = lane_half(up.shape)
    qg_hi, qg_lo = split(up[:, 64:])
    qg3 = jnp.concatenate([qg_hi, qg_lo, qg_hi], axis=1)

    def far_term(w):
        return mm(qg3, jnp.concatenate([cw_hi[w], cw_hi[w], cw_lo[w]], axis=0))

    for e in range(-FAR_CHIPS, FAR_CHIPS + 1):
        fx_send[e + FAR_CHIPS] = far_term(far_parent(e, other))
    fx_copy().start()
    far_own = [far_term(far_parent(e, core)) for e in range(-FAR_CHIPS, FAR_CHIPS + 1)]
    far_recv[2 * FAR_CHIPS] = up
    fx_copy().wait()

    def far_tile(e):
        return jnp.where(first, up, far_own[e + FAR_CHIPS] + fx_recv[e + FAR_CHIPS])

    for i, e in enumerate(far_sides):
        far_send[i] = far_tile(e)
        far_copy(i).start()
    own_tile = far_tile(0)

    for i in range(2):
        p_copy(i).wait()
        p_copy(4 + i).start()

    for c in range(clusters):
        tile_copy(c).wait()
    for i in range(2, 6):
        p_copy(i).wait()

    def near_products(c):
        def front(k, carry):
            a = table[at_block + c * slots + 2 * k]
            b = table[at_block + c * slots + 2 * k + 1]
            source = jnp.concatenate([p_win[a], p_win[b]], axis=1)
            pair = jnp.concatenate([tiles[c, 2 * k], tiles[c, 2 * k + 1]], axis=1)
            out = mm_nt(source, pair)
            for s in range(n_sub):
                pn_part[c, s] += out[:, s * quarter : (s + 1) * quarter]
            return carry

        pn_part[c] = jnp.zeros_like(pn_part[c])
        lax.fori_loop(0, slots // 2, front, 0, unroll=slots // 2)

    for c in range(clusters):
        near_products(c)
        mid_copy(c).start()
        pn_copy(1 - c, c).start()

    for step in steps:
        q_copy(step).wait()
    for c in range(clusters):
        q_rows = jnp.concatenate([q_all[s, c] for s in range(n_sub)], axis=1)

        def back(k, carry, c=c, q_rows=q_rows):
            j = c * slots + 2 * k
            pair = jnp.concatenate([tiles[c, 2 * k], tiles[c, 2 * k + 1]], axis=1)
            out = mm(q_rows, pair)
            chain[j] = out[:, :quarter] + chain[table[j]]
            chain[j + 1] = out[:, quarter:] + chain[table[j + 1]]
            return carry

        lax.fori_loop(0, slots // 2, back, 0, unroll=slots // 2)

    def back_to(parent, c):
        return chain[table[at_last + clusters * parent + c]]

    for c in range(clusters):
        q_send[2, c] = back_to(near_parent(2 * toward, other), c)
    qn_copy(2).start()
    for i, e in ((0, -toward), (2, toward), (1, 0)):
        for c in range(clusters):
            ex_send[i, c] = back_to(near_parent(e, other), c)
        ex_copy(i).start()
    ex_copy(0).wait()
    for c in range(clusters):
        q_send[0, c] = back_to(near_parent(toward, core), c) + ex_recv[0, c]
    qn_copy(0).start()

    def far_lhs(x):
        hi, lo = split(jnp.where(first, x, 0.0))
        return jnp.concatenate([hi, lo, hi], axis=1)

    def far_rhs(w):
        return jnp.concatenate([cw_hi[w], cw_hi[w], cw_lo[w]], axis=1)

    for i in range(len(far_sides)):
        far_copy(i).wait()
    ff_copy().start()
    ph = mm_nt(far_lhs(own_tile), far_rhs(far_parent(0, core)))
    total = own_tile
    for i, e in enumerate(far_sides):
        got = far_recv[i]
        ph = ph + mm_nt(far_lhs(got), far_rhs(far_parent(-e, core)))
        total = total + got
    ff_copy().wait()
    for i, e in enumerate(far_sides + (0,)):
        ph = ph + mm_nt(far_lhs(far_other[i]), far_rhs(far_parent(-e, other)))

    down_send[...] = jnp.where(first, jnp.concatenate([ph, ph], axis=1), total)
    for step in steps:
        down_copy(step).start()
    for c in range(clusters):
        mid_copy(c).wait()
        pn_part[c, peer(ways[c])] += pn_mid[c]
        pn_copy(c, c).start()
    ex_copy(2).wait()
    for c in range(clusters):
        q_send[1, c] = back_to(near_parent(-toward, core), c) + ex_recv[2, c]
    qn_copy(2).wait()
    for c in range(clusters):
        q_send[1, c] += q_recv[2, c]
    qn_copy(1).start()
    down_all[sub] = down_send[...]
    for step in steps:
        down_copy(step).wait()
    coeff = jnp.concatenate([down_all[s] for s in range(n_sub)], axis=0)
    coeff_hi, coeff_lo = split(coeff)
    coeff3 = jnp.concatenate([coeff_hi, coeff_lo, coeff_hi], axis=1)
    far_hi, far_lo = diagonal(row_hi, col_hi), diagonal(row_lo, col_lo)
    far_field = mm(coeff3, jnp.concatenate([far_hi, far_hi, far_lo], axis=0))

    ex_copy(1).wait()
    for c in range(clusters):
        half = 0.5 * mass_ref[c : c + 1]
        t_ref[c] = half * p_ref[c].astype(F32) + far_field[:, c * quarter : (c + 1) * quarter] + pn_part[c, sub]
        u = half * q_all[sub, c].astype(F32) + far_field[:, (clusters + c) * quarter : (clusters + c + 1) * quarter]
        u_ref[c] = u + (back_to(mine, c) + ex_recv[1, c])

    for c in range(clusters):
        for way in range(2):
            pn_copy(way, c).wait()
        t_ref[c] = t_ref[c] + (pn_recv[0, c] + pn_recv[1, c])
    for i in range(2):
        qn_copy(i).wait()
    for c in range(clusters):
        u_ref[c] = u_ref[c] + (q_recv[0, c] + q_recv[1, c])

    outs = [
        pltpu.make_async_copy(src, dst, out_sem.at[i]) for i, (src, dst) in enumerate(((t_ref, t_hbm), (u_ref, u_hbm)))
    ]
    for out in outs:
        out.start()

    def by_rhs(x):
        return jnp.sum(x.T, axis=0, keepdims=True)

    tt = by_rhs(t_ref[0] * t_ref[0] + t_ref[1] * t_ref[1])
    uu = by_rhs(u_ref[0] * u_ref[0] + u_ref[1] * u_ref[1])
    tu = by_rhs(t_ref[0] * u_ref[0] + t_ref[1] * u_ref[1])
    sums = jnp.concatenate([tt, uu, tu, jnp.zeros((5, rhs), F32)], axis=0)
    for g, (size, place, device) in enumerate(groups):
        ar[g, place] = sums

        def ar_copy(step, g=g, size=size, place=place, device=device):
            return pltpu.make_async_remote_copy(
                src_ref=ar.at[g, place],
                dst_ref=ar.at[g, place],
                send_sem=ar_ssem.at[g, step - 1],
                recv_sem=ar_rsem.at[g, step - 1],
                device_id=device(lax.rem(place + step, size)),
                device_id_type=MESH,
            )

        for step in range(1, size):
            ar_copy(step).start()
        for step in range(1, size):
            ar_copy(step).wait()
        sums = ar[g, 0]
        for i in range(1, size):
            sums = sums + ar[g, i]

    rho = 1.0 / jnp.sqrt(sums[0:1] + 1e-06)
    xi = 1.0 / jnp.sqrt(sums[1:2] + 1e-06)
    delta = sums[2:3] * (rho * xi)
    scale_ref[...] = jnp.concatenate([rho, xi, delta, jnp.zeros((5, rhs), F32)], axis=0)
    for out in outs:
        out.wait()


def scale_kernel(scale_ref, t_ref, u_ref, v_ref, w_ref, delta_ref):
    rhs, quarter = t_ref.shape[1:]
    v_ref[0] = t_ref[0] * jnp.broadcast_to(scale_ref[0:1], (quarter, rhs)).T
    w_ref[0] = u_ref[0] * jnp.broadcast_to(scale_ref[1:2], (quarter, rhs)).T
    delta_ref[...] = scale_ref[2:3]


def on_device(n_y, p_dir, q_dir, mass, tiles, near_ids, near_count, col, row, colt, rowt, coup, far_ids):
    clusters, rhs, quarter = p_dir.shape
    slots = tiles.shape[1]
    rank = col.shape[1]
    n_clu, n_sub = lax.axis_size("clu"), lax.axis_size("sub")
    block = rhs // n_sub
    n_keys = clusters * slots
    peers = n_sub - 1
    sides = 2 * FAR_CHIPS
    most = max(CORES * n_sub, n_y, n_clu // (n_y * CORES))
    vmem = pl.BlockSpec(memory_space=pltpu.VMEM)
    smem = pl.BlockSpec(memory_space=pltpu.SMEM)
    hbm = pl.BlockSpec(memory_space=pltpu.HBM)
    dma = pltpu.SemaphoreType.DMA
    whole = (clusters, rhs, quarter)
    t, u, scale = pl.pallas_call(
        functools.partial(kernel, (n_clu, n_sub, n_y)),
        out_shape=(
            jax.ShapeDtypeStruct(whole, F32),
            jax.ShapeDtypeStruct(whole, F32),
            jax.ShapeDtypeStruct((8, rhs), F32),
        ),
        in_specs=[smem] * 3 + [hbm] * 9,
        out_specs=(hbm, hbm, vmem),
        scratch_shapes=[
            pltpu.SMEM((2 * n_keys + clusters * NEAR_SPAN,), jnp.int32),
            pltpu.VMEM(whole, F32),
            pltpu.VMEM(whole, F32),
            pltpu.VMEM(mass.shape, F32),
            pltpu.VMEM(col.shape, BF16),
            pltpu.VMEM(col.shape, BF16),
            pltpu.VMEM(colt.shape, BF16),
            pltpu.VMEM(colt.shape, BF16),
            pltpu.VMEM(coup.shape, BF16),
            pltpu.VMEM(tiles.shape, BF16),
            pltpu.VMEM((n_sub, *whole), BF16),
            pltpu.VMEM((n_sub, rank + 16, 2 * rank), BF16),
            pltpu.VMEM((clusters * NEAR_SPAN + 1, rhs, quarter), BF16),
            pltpu.VMEM((rhs, 2 * rank), F32),
            pltpu.VMEM((peers, block, 2 * rank), F32),
            pltpu.VMEM((FAR_SPAN, rank, 2 * rank), BF16),
            pltpu.VMEM((FAR_SPAN, rank, 2 * rank), BF16),
            pltpu.VMEM((sides + 1, block, 2 * rank), F32),
            pltpu.VMEM((sides + 1, block, 2 * rank), F32),
            pltpu.VMEM((sides, block, 2 * rank), F32),
            pltpu.VMEM((sides + 1, block, 2 * rank), F32),
            pltpu.VMEM((sides + 1, block, 2 * rank), F32),
            pltpu.VMEM((n_keys + 1, rhs, quarter), F32),
            pltpu.VMEM((3, *whole), F32),
            pltpu.VMEM((3, *whole), F32),
            pltpu.VMEM((3, *whole), F32),
            pltpu.VMEM((3, *whole), F32),
            pltpu.VMEM((clusters, n_sub, rhs, quarter), F32),
            pltpu.VMEM(whole, F32),
            pltpu.VMEM((2, *whole), F32),
            pltpu.VMEM((block, 2 * rank), F32),
            pltpu.VMEM((n_sub, block, 2 * rank), F32),
            pltpu.VMEM((3, most, 8, rhs), F32),
            dma((2,)),
            dma((8,)),
            dma((clusters,)),
            dma((peers,)),
            dma((peers,)),
            dma((peers,)),
            dma((peers,)),
            dma((6,)),
            dma((6,)),
            dma((peers,)),
            dma((peers,)),
            dma((2,)),
            dma((sides,)),
            dma((sides,)),
            dma((2,)),
            dma((2, 3)),
            dma((3,)),
            dma((3,)),
            dma((2, clusters)),
            dma((2, clusters)),
            dma((2, clusters)),
            dma((peers,)),
            dma((peers,)),
            dma((3, most)),
            dma((3, most)),
        ],
        compiler_params=pltpu.CompilerParams(
            collective_id=0, has_side_effects=True, vmem_limit_bytes=VMEM_BYTES
        ),
    )(near_ids, near_count, far_ids, p_dir, q_dir, mass, col, row, colt, rowt, coup, tiles)
    one = pl.BlockSpec((1, rhs, quarter), lambda c: (c, 0, 0))
    v, w, delta = pl.pallas_call(
        scale_kernel,
        grid=(clusters,),
        out_shape=(
            jax.ShapeDtypeStruct(whole, F32),
            jax.ShapeDtypeStruct(whole, F32),
            jax.ShapeDtypeStruct((1, rhs), F32),
        ),
        in_specs=[pl.BlockSpec((8, rhs), lambda c: (0, 0)), one, one],
        out_specs=(one, one, pl.BlockSpec((1, rhs), lambda c: (0, 0))),
        compiler_params=pltpu.CompilerParams(vmem_limit_bytes=VMEM_BYTES),
    )(scale, t, u)
    return v, w, delta.reshape(rhs)


def build(mesh, n_y):
    return jax.shard_map(
        functools.partial(on_device, n_y),
        mesh=mesh,
        in_specs=(
            P("clu", None, "sub"),
            P("clu", None, "sub"),
            P("clu", "sub"),
            P("clu", None, None, "sub"),
            P("clu", None),
            P("clu"),
            P("clu", None, "sub"),
            P("clu", None, "sub"),
            P("clu", None, None),
            P("clu", None, None),
            P("clu", "sub", None, None),
            P("clu", "sub"),
        ),
        out_specs=(P("clu", None, "sub"), P("clu", None, "sub"), P()),
        check_vma=False,
    )


def solution(mesh):
    return build(mesh, CHIPS_Y)
```

```python
import functools

import jax
import jax.numpy as jnp
from jax import lax
from jax.experimental import pallas as pl
from jax.experimental.pallas import tpu as pltpu
from jax.sharding import PartitionSpec as P

CORES = 2
CHIPS_Y = 8
NEAR_CHIPS = 2
FAR_CHIPS = 3
VMEM_BYTES = 64 * 1024 * 1024 - 64 * 1024
MESH = pl.DeviceIdType.MESH
F32 = jnp.float32
BF16 = jnp.bfloat16
NEAR_SPAN = CORES * (2 * NEAR_CHIPS + 1)
FAR_SPAN = CORES * (2 * FAR_CHIPS + 1)


def mm(a, b):
    return lax.dot_general(a, b, (((1,), (0,)), ((), ())), preferred_element_type=F32)


def mm_nt(a, b):
    return lax.dot_general(a, b, (((1,), (1,)), ((), ())), preferred_element_type=F32)


def mm_tn(a, b):
    return lax.dot_general(a, b, (((0,), (0,)), ((), ())), preferred_element_type=F32)


def split(x):
    hi = x.astype(BF16)
    return hi, (x - hi.astype(F32)).astype(BF16)


def lane_half(shape):
    return lax.broadcasted_iota(jnp.int32, shape, 1) < shape[1] // 2


def kernel(
    sizes,
    ids_ref,
    count_ref,
    far_ref,
    p_hbm,
    q_hbm,
    mass_hbm,
    col_hbm,
    row_hbm,
    colt_hbm,
    rowt_hbm,
    coup_hbm,
    tiles_hbm,
    t_hbm,
    u_hbm,
    scale_ref,
    table,
    t_ref,
    u_ref,
    mass_ref,
    col_ref,
    row_ref,
    colt_ref,
    rowt_ref,
    coup_ref,
    tiles,
    q_all,
    coup_all,
    p_win,
    up_part,
    up_recv,
    cw_hi,
    cw_lo,
    fx_send,
    fx_recv,
    far_send,
    far_recv,
    far_other,
    chain,
    ex_send,
    ex_recv,
    q_send,
    q_recv,
    pn_part,
    pn_mid,
    pn_recv,
    down_send,
    down_all,
    ar,
    out_sem,
    load_sem,
    tile_sem,
    q_ssem,
    q_rsem,
    c_ssem,
    c_rsem,
    p_ssem,
    p_rsem,
    up_ssem,
    up_rsem,
    fx_sem,
    far_ssem,
    far_rsem,
    ff_sem,
    ex_sem,
    qn_ssem,
    qn_rsem,
    mid_sem,
    pn_ssem,
    pn_rsem,
    down_ssem,
    down_rsem,
    ar_ssem,
    ar_rsem,
):
    n_clu, n_sub, n_y = sizes
    n_chips = n_clu // CORES
    n_z = n_chips // n_y
    clu = lax.axis_index("clu")
    sub = lax.axis_index("sub")
    core = lax.rem(clu, CORES)
    other = 1 - core
    chip = clu // CORES
    y = lax.rem(chip, n_y)
    z = chip // n_y
    toward = 2 * core - 1
    _, clusters, rhs, quarter = q_all.shape
    slots = tiles.shape[1]
    block = rhs // n_sub

    def on_chip(offset, which):
        return (lax.rem(chip + (offset + n_chips), n_chips) * CORES + which, sub)

    def peer(step):
        return lax.rem(sub + step, n_sub)

    sibling = (chip * CORES + other, sub)

    groups = (
        (CORES * n_sub, sub * CORES + core, lambda i: (chip * CORES + lax.rem(i, CORES), i // CORES)),
        (n_y, y, lambda i: ((z * n_y + i) * CORES + core, sub)),
        (n_z, z, lambda i: ((i * n_y + y) * CORES + core, sub)),
    )

    def near_parent(offset, which):
        return 2 * (NEAR_CHIPS + offset) + which

    def far_parent(offset, which):
        return 2 * (FAR_CHIPS + offset) + which

    def window(parent):
        return p_win.at[pl.ds(parent * clusters, clusters)]

    mine = near_parent(0, core)
    p_ref = window(mine)
    loads = [
        pltpu.make_async_copy(src, dst, load_sem.at[i])
        for i, (src, dst) in enumerate(
            (
                (q_hbm, q_all.at[sub]),
                (p_hbm, p_ref),
                (col_hbm, col_ref),
                (row_hbm, row_ref),
                (colt_hbm, colt_ref),
                (rowt_hbm, rowt_ref),
                (coup_hbm, coup_ref),
                (mass_hbm, mass_ref),
            )
        )
    ]

    def tile_copy(c):
        return pltpu.make_async_copy(tiles_hbm.at[c], tiles.at[c], tile_sem.at[c])

    for load in loads[:6]:
        load.start()

    barrier = pltpu.get_barrier_semaphore()
    partners = [
        (min(step, size - step), device(lax.rem(place + step, size)))
        for size, place, device in groups
        for step in range(1, size)
    ]
    partners += [(k, on_chip(d, core)) for k in range(1, FAR_CHIPS + 1) for d in (-k, k)]
    partners += [(d, on_chip(d * toward, other)) for d in (1, 2)]
    for _, partner in sorted(partners, key=lambda entry: -entry[0]):
        pl.semaphore_signal(barrier, inc=1, device_id=partner, device_id_type=MESH)

    for load in loads[6:]:
        load.start()
    for c in range(clusters):
        tile_copy(c).start()

    n_keys = clusters * slots
    empty = p_win.shape[0] - 1
    at_last = n_keys
    at_block = n_keys + empty
    base = (chip - NEAR_CHIPS) * (CORES * clusters)
    for c in range(clusters):
        for s in range(slots):
            table[at_block + c * slots + s] = jnp.where(s < count_ref[c], ids_ref[c, s] - base, empty)

    def find(j, carry):
        wanted = table[at_block + j]
        found = jnp.int32(n_keys)
        for i in range(n_keys):
            found = jnp.where((table[at_block + i] == wanted) & (i < j), i, found)
        table[j] = found
        return carry

    def find_last(w, carry):
        found = jnp.int32(n_keys)
        for i in range(n_keys):
            found = jnp.where(table[at_block + i] == w, i, found)
        table[at_last + w] = found
        return carry

    p_win[empty] = jnp.zeros((rhs, quarter), BF16)
    chain[n_keys] = jnp.zeros((rhs, quarter), F32)
    for load in loads:
        load.wait()

    rank = coup_ref.shape[2]
    far_base = (chip - FAR_CHIPS) * CORES
    coup_all[sub, :rank] = jnp.concatenate([coup_ref[0, 0], coup_ref[0, 1]], axis=1)
    places = jnp.where(lane_half((16, 2 * rank)), far_ref[0, 0] - far_base, far_ref[0, 1] - far_base)
    coup_all[sub, rank:] = places.astype(F32).astype(BF16)

    cols = [split(mm_tn(colt_ref[c], col_ref[c])) for c in range(clusters)]
    rows = [split(mm_tn(rowt_ref[c], row_ref[c])) for c in range(clusters)]
    none = jnp.zeros((cols[0][0].shape[0], clusters * quarter), BF16)
    col_hi, col_lo = (jnp.concatenate([x[k] for x in cols], axis=1) for k in range(2))
    row_hi, row_lo = (jnp.concatenate([x[k] for x in rows], axis=1) for k in range(2))

    def diagonal(a, b):
        return jnp.concatenate([jnp.concatenate([a, none], axis=1), jnp.concatenate([none, b], axis=1)], axis=0)

    both = jnp.concatenate([p_ref[0], p_ref[1], q_all[sub, 0], q_all[sub, 1]], axis=1)
    up_part[...] = mm_nt(both, diagonal(col_hi, row_hi)) + mm_nt(both, diagonal(col_lo, row_lo))

    pl.semaphore_wait(barrier, len(partners))

    def remote(src, dst, ssem, rsem, device):
        return pltpu.make_async_remote_copy(
            src_ref=src, dst_ref=dst, send_sem=ssem, recv_sem=rsem, device_id=device, device_id_type=MESH
        )

    def to_peer(src, dst, ssem, rsem, step):
        return remote(src, dst, ssem, rsem, (clu, peer(step)))

    def q_copy(step, c):
        own = q_all.at[sub, c]
        return to_peer(own, own, q_ssem.at[step - 1, c], q_rsem.at[step - 1, c], step)

    def c_copy(step):
        return to_peer(coup_all.at[sub], coup_all.at[sub], c_ssem.at[step - 1], c_rsem.at[step - 1], step)

    def up_copy(step):
        rows = pl.ds(pl.multiple_of(peer(step) * block, block), block)
        return to_peer(up_part.at[rows], up_recv.at[step - 1], up_ssem.at[step - 1], up_rsem.at[step - 1], step)

    def down_copy(step):
        return to_peer(down_send, down_all.at[sub], down_ssem.at[step - 1], down_rsem.at[step - 1], step)

    ways = (1, n_sub - 1)

    def mid_copy(c):
        return to_peer(pn_part.at[c, peer(2)], pn_mid.at[c], mid_sem.at[0, c], mid_sem.at[1, c], ways[c])

    def pn_copy(way, c):
        return to_peer(
            pn_part.at[c, peer(ways[way])], pn_recv.at[way, c], pn_ssem.at[way, c], pn_rsem.at[way, c], ways[way]
        )

    sides = (1, -1)

    def p_copy(i):
        if i < 2:
            source, there, device = mine, near_parent(-sides[i], core), on_chip(sides[i], core)
        elif i == 2:
            source, there, device = mine, near_parent(-2 * toward, core), on_chip(2 * toward, other)
        elif i == 3:
            source, there, device = mine, mine, sibling
        else:
            source = there = near_parent(-sides[i - 4], core)
            device = sibling
        return remote(window(source), window(there), p_ssem.at[i], p_rsem.at[i], device)

    far_sides = tuple(d for k in range(FAR_CHIPS, 0, -1) for d in (k, -k))

    def fx_copy():
        return remote(fx_send, fx_recv, fx_sem.at[0], fx_sem.at[1], sibling)

    def far_copy(i):
        return remote(far_send.at[i], far_recv.at[i], far_ssem.at[i], far_rsem.at[i], on_chip(far_sides[i], core))

    def ff_copy():
        return remote(far_recv, far_other, ff_sem.at[0], ff_sem.at[1], sibling)

    def ex_copy(i):
        return remote(ex_send.at[i], ex_recv.at[i], ex_sem.at[0, i], ex_sem.at[1, i], sibling)

    def qn_copy(i, c):
        device = (on_chip(toward, core), on_chip(-toward, core), on_chip(toward, other))[i]
        return remote(q_send.at[i, c], q_recv.at[i, c], qn_ssem.at[i, c], qn_rsem.at[i, c], device)

    steps = range(1, n_sub)
    far_first = sorted(steps, key=lambda step: -min(step, n_sub - step))
    for step in far_first:
        up_copy(step).start()
    for i in (2, 0, 1, 3):
        p_copy(i).start()
    for step in far_first:
        c_copy(step).start()
    for c in range(clusters):
        for step in far_first:
            q_copy(step, c).start()

    lax.fori_loop(0, n_keys, find, 0)
    lax.fori_loop(0, empty, find_last, 0)

    for step in steps:
        c_copy(step).wait()

    def gather_offset(w, carry):
        total = jnp.zeros((rank, 2 * rank), F32)
        for s in range(n_sub):
            here = coup_all[s, rank : rank + 1].astype(F32) == w.astype(F32)
            total = total + jnp.where(here, coup_all[s, :rank].astype(F32), 0.0)
        hi, lo = split(total + jnp.concatenate([total[:, rank:], total[:, :rank]], axis=1))
        cw_hi[w] = hi
        cw_lo[w] = lo
        return carry

    lax.fori_loop(0, FAR_SPAN, gather_offset, 0)

    for step in steps:
        up_copy(step).wait()
    up = up_part[pl.ds(pl.multiple_of(sub * block, block), block)]
    for step in steps:
        up = up + up_recv[step - 1]
    first = lane_half(up.shape)
    qg_hi, qg_lo = split(up[:, 64:])
    qg3 = jnp.concatenate([qg_hi, qg_lo, qg_hi], axis=1)

    def far_term(w):
        return mm(qg3, jnp.concatenate([cw_hi[w], cw_hi[w], cw_lo[w]], axis=0))

    for e in range(-FAR_CHIPS, FAR_CHIPS + 1):
        fx_send[e + FAR_CHIPS] = far_term(far_parent(e, other))
    fx_copy().start()
    far_own = [far_term(far_parent(e, core)) for e in range(-FAR_CHIPS, FAR_CHIPS + 1)]
    far_recv[2 * FAR_CHIPS] = up
    fx_copy().wait()

    def far_tile(e):
        return jnp.where(first, up, far_own[e + FAR_CHIPS] + fx_recv[e + FAR_CHIPS])

    for i, e in enumerate(far_sides):
        far_send[i] = far_tile(e)
        far_copy(i).start()
    own_tile = far_tile(0)

    for i in range(2):
        p_copy(i).wait()
        p_copy(4 + i).start()

    for c in range(clusters):
        tile_copy(c).wait()
    for i in range(2, 6):
        p_copy(i).wait()

    def near_products(c):
        def front(k, carry):
            a = table[at_block + c * slots + 2 * k]
            b = table[at_block + c * slots + 2 * k + 1]
            source = jnp.concatenate([p_win[a], p_win[b]], axis=1)
            pair = jnp.concatenate([tiles[c, 2 * k], tiles[c, 2 * k + 1]], axis=1)
            out = mm_nt(source, pair)
            for s in range(n_sub):
                pn_part[c, s] += out[:, s * quarter : (s + 1) * quarter]
            return carry

        pn_part[c] = jnp.zeros_like(pn_part[c])
        lax.fori_loop(0, slots // 2, front, 0, unroll=slots // 2)

    for c in range(clusters):
        near_products(c)
        mid_copy(c).start()
        pn_copy(1 - c, c).start()

    for c in range(clusters):
        for step in steps:
            q_copy(step, c).wait()
        q_rows = jnp.concatenate([q_all[s, c] for s in range(n_sub)], axis=1)

        def back(k, carry, c=c, q_rows=q_rows):
            j = c * slots + 2 * k
            pair = jnp.concatenate([tiles[c, 2 * k], tiles[c, 2 * k + 1]], axis=1)
            out = mm(q_rows, pair)
            chain[j] = out[:, :quarter] + chain[table[j]]
            chain[j + 1] = out[:, quarter:] + chain[table[j + 1]]
            return carry

        lax.fori_loop(0, slots // 2, back, 0, unroll=slots // 2)

    def back_to(parent, c):
        return chain[table[at_last + clusters * parent + c]]

    for c in range(clusters):
        q_send[2, c] = back_to(near_parent(2 * toward, other), c)
        qn_copy(2, c).start()
    for i, e in ((0, -toward), (2, toward), (1, 0)):
        for c in range(clusters):
            ex_send[i, c] = back_to(near_parent(e, other), c)
        ex_copy(i).start()
    ex_copy(0).wait()
    for c in range(clusters):
        q_send[0, c] = back_to(near_parent(toward, core), c) + ex_recv[0, c]
        qn_copy(0, c).start()

    def far_lhs(x):
        hi, lo = split(jnp.where(first, x, 0.0))
        return jnp.concatenate([hi, lo, hi], axis=1)

    def far_rhs(w):
        return jnp.concatenate([cw_hi[w], cw_hi[w], cw_lo[w]], axis=1)

    for i in range(len(far_sides)):
        far_copy(i).wait()
    ff_copy().start()
    ph = mm_nt(far_lhs(own_tile), far_rhs(far_parent(0, core)))
    total = own_tile
    for i, e in enumerate(far_sides):
        got = far_recv[i]
        ph = ph + mm_nt(far_lhs(got), far_rhs(far_parent(-e, core)))
        total = total + got
    ff_copy().wait()
    for i, e in enumerate(far_sides + (0,)):
        ph = ph + mm_nt(far_lhs(far_other[i]), far_rhs(far_parent(-e, other)))

    down_send[...] = jnp.where(first, jnp.concatenate([ph, ph], axis=1), total)
    for step in far_first:
        down_copy(step).start()
    ex_copy(2).wait()
    for c in range(clusters):
        q_send[1, c] = back_to(near_parent(-toward, core), c) + ex_recv[2, c]
    for c in range(clusters):
        qn_copy(2, c).wait()
        q_send[1, c] += q_recv[2, c]
        qn_copy(1, c).start()
    for c in range(clusters):
        mid_copy(c).wait()
        pn_part[c, peer(ways[c])] += pn_mid[c]
        pn_copy(c, c).start()
    down_all[sub] = down_send[...]
    for step in steps:
        down_copy(step).wait()
    coeff = jnp.concatenate([down_all[s] for s in range(n_sub)], axis=0)
    coeff_hi, coeff_lo = split(coeff)
    coeff3 = jnp.concatenate([coeff_hi, coeff_lo, coeff_hi], axis=1)
    far_hi, far_lo = diagonal(row_hi, col_hi), diagonal(row_lo, col_lo)
    far_field = mm(coeff3, jnp.concatenate([far_hi, far_hi, far_lo], axis=0))

    ex_copy(1).wait()
    for c in range(clusters):
        half = 0.5 * mass_ref[c : c + 1]
        t_ref[c] = half * p_ref[c].astype(F32) + far_field[:, c * quarter : (c + 1) * quarter] + pn_part[c, sub]
        u = half * q_all[sub, c].astype(F32) + far_field[:, (clusters + c) * quarter : (clusters + c + 1) * quarter]
        u_ref[c] = u + (back_to(mine, c) + ex_recv[1, c])

    for c in range(clusters):
        for way in range(2):
            pn_copy(way, c).wait()
        t_ref[c] = t_ref[c] + (pn_recv[0, c] + pn_recv[1, c])
    for c in range(clusters):
        for i in range(2):
            qn_copy(i, c).wait()
        u_ref[c] = u_ref[c] + (q_recv[0, c] + q_recv[1, c])

    outs = [
        pltpu.make_async_copy(src, dst, out_sem.at[i]) for i, (src, dst) in enumerate(((t_ref, t_hbm), (u_ref, u_hbm)))
    ]
    for out in outs:
        out.start()

    def by_rhs(x):
        return jnp.sum(x.T, axis=0, keepdims=True)

    half_rhs = rhs // 2
    tt = by_rhs(t_ref[0] * t_ref[0] + t_ref[1] * t_ref[1])
    uu = by_rhs(u_ref[0] * u_ref[0] + u_ref[1] * u_ref[1])
    tu = by_rhs(t_ref[0] * u_ref[0] + t_ref[1] * u_ref[1])
    halves = [x[:, k * half_rhs : (k + 1) * half_rhs] for x in (tt, uu, tu) for k in range(2)]
    sums = jnp.concatenate(halves + [jnp.zeros((2, half_rhs), F32)], axis=0)
    for g, (size, place, device) in enumerate(groups):
        ar[g, place] = sums

        def ar_copy(step, g=g, size=size, place=place, device=device):
            return pltpu.make_async_remote_copy(
                src_ref=ar.at[g, place],
                dst_ref=ar.at[g, place],
                send_sem=ar_ssem.at[g, step - 1],
                recv_sem=ar_rsem.at[g, step - 1],
                device_id=device(lax.rem(place + step, size)),
                device_id_type=MESH,
            )

        for step in range(1, size):
            ar_copy(step).start()
        for step in range(1, size):
            ar_copy(step).wait()
        sums = ar[g, 0]
        for i in range(1, size):
            sums = sums + ar[g, i]

    rho = 1.0 / jnp.sqrt(sums[0:2] + 1e-06)
    xi = 1.0 / jnp.sqrt(sums[2:4] + 1e-06)
    delta = sums[4:6] * (rho * xi)
    scale_ref[...] = jnp.concatenate([rho, xi, delta, jnp.zeros((2, half_rhs), F32)], axis=0)
    for out in outs:
        out.wait()


def scale_kernel(scale_ref, t_ref, u_ref, v_ref, w_ref, delta_ref):
    _, rhs, quarter = t_ref.shape
    half_rhs = rhs // 2
    for k, (src, dst) in enumerate(((t_ref, v_ref), (u_ref, w_ref))):
        for h in range(2):
            rows = slice(h * half_rhs, (h + 1) * half_rhs)
            factor = scale_ref[2 * k + h : 2 * k + h + 1]
            dst[0, rows] = src[0, rows] * jnp.broadcast_to(factor, (quarter, half_rhs)).T
    delta_ref[...] = jnp.concatenate([scale_ref[4:5], scale_ref[5:6]], axis=1)


def on_device(n_y, p_dir, q_dir, mass, tiles, near_ids, near_count, col, row, colt, rowt, coup, far_ids):
    clusters, rhs, quarter = p_dir.shape
    slots = tiles.shape[1]
    rank = col.shape[1]
    n_clu, n_sub = lax.axis_size("clu"), lax.axis_size("sub")
    block = rhs // n_sub
    n_keys = clusters * slots
    peers = n_sub - 1
    sides = 2 * FAR_CHIPS
    most = max(CORES * n_sub, n_y, n_clu // (n_y * CORES))
    vmem = pl.BlockSpec(memory_space=pltpu.VMEM)
    smem = pl.BlockSpec(memory_space=pltpu.SMEM)
    hbm = pl.BlockSpec(memory_space=pltpu.HBM)
    dma = pltpu.SemaphoreType.DMA
    whole = (clusters, rhs, quarter)
    t, u, scale = pl.pallas_call(
        functools.partial(kernel, (n_clu, n_sub, n_y)),
        out_shape=(
            jax.ShapeDtypeStruct(whole, F32),
            jax.ShapeDtypeStruct(whole, F32),
            jax.ShapeDtypeStruct((8, rhs // 2), F32),
        ),
        in_specs=[smem] * 3 + [hbm] * 9,
        out_specs=(hbm, hbm, vmem),
        scratch_shapes=[
            pltpu.SMEM((2 * n_keys + clusters * NEAR_SPAN,), jnp.int32),
            pltpu.VMEM(whole, F32),
            pltpu.VMEM(whole, F32),
            pltpu.VMEM(mass.shape, F32),
            pltpu.VMEM(col.shape, BF16),
            pltpu.VMEM(col.shape, BF16),
            pltpu.VMEM(colt.shape, BF16),
            pltpu.VMEM(colt.shape, BF16),
            pltpu.VMEM(coup.shape, BF16),
            pltpu.VMEM(tiles.shape, BF16),
            pltpu.VMEM((n_sub, *whole), BF16),
            pltpu.VMEM((n_sub, rank + 16, 2 * rank), BF16),
            pltpu.VMEM((clusters * NEAR_SPAN + 1, rhs, quarter), BF16),
            pltpu.VMEM((rhs, 2 * rank), F32),
            pltpu.VMEM((peers, block, 2 * rank), F32),
            pltpu.VMEM((FAR_SPAN, rank, 2 * rank), BF16),
            pltpu.VMEM((FAR_SPAN, rank, 2 * rank), BF16),
            pltpu.VMEM((sides + 1, block, 2 * rank), F32),
            pltpu.VMEM((sides + 1, block, 2 * rank), F32),
            pltpu.VMEM((sides, block, 2 * rank), F32),
            pltpu.VMEM((sides + 1, block, 2 * rank), F32),
            pltpu.VMEM((sides + 1, block, 2 * rank), F32),
            pltpu.VMEM((n_keys + 1, rhs, quarter), F32),
            pltpu.VMEM((3, *whole), F32),
            pltpu.VMEM((3, *whole), F32),
            pltpu.VMEM((3, *whole), F32),
            pltpu.VMEM((3, *whole), F32),
            pltpu.VMEM((clusters, n_sub, rhs, quarter), F32),
            pltpu.VMEM(whole, F32),
            pltpu.VMEM((2, *whole), F32),
            pltpu.VMEM((block, 2 * rank), F32),
            pltpu.VMEM((n_sub, block, 2 * rank), F32),
            pltpu.VMEM((3, most, 8, rhs // 2), F32),
            dma((2,)),
            dma((8,)),
            dma((clusters,)),
            dma((peers, clusters)),
            dma((peers, clusters)),
            dma((peers,)),
            dma((peers,)),
            dma((6,)),
            dma((6,)),
            dma((peers,)),
            dma((peers,)),
            dma((2,)),
            dma((sides,)),
            dma((sides,)),
            dma((2,)),
            dma((2, 3)),
            dma((3, clusters)),
            dma((3, clusters)),
            dma((2, clusters)),
            dma((2, clusters)),
            dma((2, clusters)),
            dma((peers,)),
            dma((peers,)),
            dma((3, most)),
            dma((3, most)),
        ],
        compiler_params=pltpu.CompilerParams(
            collective_id=0, has_side_effects=True, vmem_limit_bytes=VMEM_BYTES
        ),
    )(near_ids, near_count, far_ids, p_dir, q_dir, mass, col, row, colt, rowt, coup, tiles)
    one = pl.BlockSpec((1, rhs, quarter), lambda c: (c, 0, 0))
    v, w, delta = pl.pallas_call(
        scale_kernel,
        grid=(clusters,),
        out_shape=(
            jax.ShapeDtypeStruct(whole, F32),
            jax.ShapeDtypeStruct(whole, F32),
            jax.ShapeDtypeStruct((1, rhs), F32),
        ),
        in_specs=[pl.BlockSpec((8, rhs // 2), lambda c: (0, 0)), one, one],
        out_specs=(one, one, pl.BlockSpec((1, rhs), lambda c: (0, 0))),
        compiler_params=pltpu.CompilerParams(vmem_limit_bytes=VMEM_BYTES),
    )(scale, t, u)
    return v, w, delta.reshape(rhs)


def build(mesh, n_y):
    return jax.shard_map(
        functools.partial(on_device, n_y),
        mesh=mesh,
        in_specs=(
            P("clu", None, "sub"),
            P("clu", None, "sub"),
            P("clu", "sub"),
            P("clu", None, None, "sub"),
            P("clu", None),
            P("clu"),
            P("clu", None, "sub"),
            P("clu", None, "sub"),
            P("clu", None, None),
            P("clu", None, None),
            P("clu", "sub", None, None),
            P("clu", "sub"),
        ),
        out_specs=(P("clu", None, "sub"), P("clu", None, "sub"), P()),
        check_vma=False,
    )


def solution(mesh):
    return build(mesh, CHIPS_Y)
```

```python
import functools

import jax
import jax.numpy as jnp
from jax import lax
from jax.experimental import pallas as pl
from jax.experimental.pallas import tpu as pltpu
from jax.sharding import PartitionSpec as P

CORES = 2
CHIPS_Y = 8
NEAR_CHIPS = 2
FAR_CHIPS = 3
VMEM_BYTES = 64 * 1024 * 1024 - 64 * 1024
MESH = pl.DeviceIdType.MESH
F32 = jnp.float32
BF16 = jnp.bfloat16
NEAR_SPAN = CORES * (2 * NEAR_CHIPS + 1)
FAR_SPAN = CORES * (2 * FAR_CHIPS + 1)


def mm(a, b):
    return lax.dot_general(a, b, (((1,), (0,)), ((), ())), preferred_element_type=F32)


def mm_nt(a, b):
    return lax.dot_general(a, b, (((1,), (1,)), ((), ())), preferred_element_type=F32)


def mm_tn(a, b):
    return lax.dot_general(a, b, (((0,), (0,)), ((), ())), preferred_element_type=F32)


def split(x):
    hi = x.astype(BF16)
    return hi, (x - hi.astype(F32)).astype(BF16)


def lane_half(shape):
    return lax.broadcasted_iota(jnp.int32, shape, 1) < shape[1] // 2


def kernel(
    sizes,
    ids_ref,
    count_ref,
    far_ref,
    p_hbm,
    q_hbm,
    mass_hbm,
    col_hbm,
    row_hbm,
    colt_hbm,
    rowt_hbm,
    coup_hbm,
    tiles_hbm,
    t_hbm,
    u_hbm,
    scale_ref,
    table,
    t_ref,
    u_ref,
    mass_ref,
    col_ref,
    row_ref,
    colt_ref,
    rowt_ref,
    coup_ref,
    tiles,
    q_all,
    coup_all,
    p_win,
    up_part,
    up_recv,
    cw_hi,
    cw_lo,
    fx_send,
    fx_recv,
    far_send,
    far_recv,
    far_other,
    chain,
    ex_send,
    ex_recv,
    q_send,
    q_recv,
    pn_part,
    pn_mid,
    pn_recv,
    down_send,
    down_all,
    ar,
    out_sem,
    load_sem,
    tile_sem,
    q_ssem,
    q_rsem,
    c_ssem,
    c_rsem,
    p_ssem,
    p_rsem,
    up_ssem,
    up_rsem,
    fx_sem,
    far_ssem,
    far_rsem,
    ff_sem,
    ex_sem,
    qn_ssem,
    qn_rsem,
    mid_sem,
    pn_ssem,
    pn_rsem,
    down_ssem,
    down_rsem,
    ar_ssem,
    ar_rsem,
):
    n_clu, n_sub, n_y = sizes
    n_chips = n_clu // CORES
    n_z = n_chips // n_y
    clu = lax.axis_index("clu")
    sub = lax.axis_index("sub")
    core = lax.rem(clu, CORES)
    other = 1 - core
    chip = clu // CORES
    y = lax.rem(chip, n_y)
    z = chip // n_y
    toward = 2 * core - 1
    _, clusters, rhs, quarter = q_all.shape
    slots = tiles.shape[1]
    block = rhs // n_sub

    def on_chip(offset, which):
        return (lax.rem(chip + (offset + n_chips), n_chips) * CORES + which, sub)

    def peer(step):
        return lax.rem(sub + step, n_sub)

    sibling = (chip * CORES + other, sub)

    groups = (
        (CORES * n_sub, sub * CORES + core, lambda i: (chip * CORES + lax.rem(i, CORES), i // CORES)),
        (n_y, y, lambda i: ((z * n_y + i) * CORES + core, sub)),
        (n_z, z, lambda i: ((i * n_y + y) * CORES + core, sub)),
    )

    def near_parent(offset, which):
        return 2 * (NEAR_CHIPS + offset) + which

    def far_parent(offset, which):
        return 2 * (FAR_CHIPS + offset) + which

    def window(parent):
        return p_win.at[pl.ds(parent * clusters, clusters)]

    mine = near_parent(0, core)
    p_ref = window(mine)
    loads = [
        pltpu.make_async_copy(src, dst, load_sem.at[i])
        for i, (src, dst) in enumerate(
            (
                (q_hbm, q_all.at[sub]),
                (p_hbm, p_ref),
                (col_hbm, col_ref),
                (row_hbm, row_ref),
                (colt_hbm, colt_ref),
                (rowt_hbm, rowt_ref),
                (coup_hbm, coup_ref),
                (mass_hbm, mass_ref),
            )
        )
    ]

    def tile_copy(c):
        return pltpu.make_async_copy(tiles_hbm.at[c], tiles.at[c], tile_sem.at[c])

    for load in loads[:6]:
        load.start()

    barrier = pltpu.get_barrier_semaphore()
    partners = [
        (min(step, size - step), device(lax.rem(place + step, size)))
        for size, place, device in groups
        for step in range(1, size)
    ]
    partners += [(k, on_chip(d, core)) for k in range(1, FAR_CHIPS + 1) for d in (-k, k)]
    partners += [(d, on_chip(d * toward, other)) for d in (1, 2)]
    for _, partner in sorted(partners, key=lambda entry: -entry[0]):
        pl.semaphore_signal(barrier, inc=1, device_id=partner, device_id_type=MESH)

    for load in loads[6:]:
        load.start()
    for c in range(clusters):
        tile_copy(c).start()

    n_keys = clusters * slots
    empty = p_win.shape[0] - 1
    at_last = n_keys
    at_block = n_keys + empty
    base = (chip - NEAR_CHIPS) * (CORES * clusters)
    for c in range(clusters):
        for s in range(slots):
            table[at_block + c * slots + s] = jnp.where(s < count_ref[c], ids_ref[c, s] - base, empty)

    def find(j, carry):
        wanted = table[at_block + j]
        found = jnp.int32(n_keys)
        for i in range(n_keys):
            found = jnp.where((table[at_block + i] == wanted) & (i < j), i, found)
        table[j] = found
        return carry

    def find_last(w, carry):
        found = jnp.int32(n_keys)
        for i in range(n_keys):
            found = jnp.where(table[at_block + i] == w, i, found)
        table[at_last + w] = found
        return carry

    p_win[empty] = jnp.zeros((rhs, quarter), BF16)
    chain[n_keys] = jnp.zeros((rhs, quarter), F32)
    for load in loads:
        load.wait()

    rank = coup_ref.shape[2]
    far_base = (chip - FAR_CHIPS) * CORES
    coup_all[sub, :rank] = jnp.concatenate([coup_ref[0, 0], coup_ref[0, 1]], axis=1)
    places = jnp.where(lane_half((16, 2 * rank)), far_ref[0, 0] - far_base, far_ref[0, 1] - far_base)
    coup_all[sub, rank:] = places.astype(F32).astype(BF16)

    cols = [split(mm_tn(colt_ref[c], col_ref[c])) for c in range(clusters)]
    rows = [split(mm_tn(rowt_ref[c], row_ref[c])) for c in range(clusters)]
    none = jnp.zeros((cols[0][0].shape[0], clusters * quarter), BF16)
    col_hi, col_lo = (jnp.concatenate([x[k] for x in cols], axis=1) for k in range(2))
    row_hi, row_lo = (jnp.concatenate([x[k] for x in rows], axis=1) for k in range(2))

    def diagonal(a, b):
        return jnp.concatenate([jnp.concatenate([a, none], axis=1), jnp.concatenate([none, b], axis=1)], axis=0)

    both = jnp.concatenate([p_ref[0], p_ref[1], q_all[sub, 0], q_all[sub, 1]], axis=1)
    up_part[...] = mm_nt(both, diagonal(col_hi, row_hi)) + mm_nt(both, diagonal(col_lo, row_lo))

    pl.semaphore_wait(barrier, len(partners))

    def remote(src, dst, ssem, rsem, device):
        return pltpu.make_async_remote_copy(
            src_ref=src, dst_ref=dst, send_sem=ssem, recv_sem=rsem, device_id=device, device_id_type=MESH
        )

    def to_peer(src, dst, ssem, rsem, step):
        return remote(src, dst, ssem, rsem, (clu, peer(step)))

    def q_copy(step, c):
        own = q_all.at[sub, c]
        return to_peer(own, own, q_ssem.at[step - 1, c], q_rsem.at[step - 1, c], step)

    def c_copy(step):
        return to_peer(coup_all.at[sub], coup_all.at[sub], c_ssem.at[step - 1], c_rsem.at[step - 1], step)

    def up_copy(step):
        rows = pl.ds(pl.multiple_of(peer(step) * block, block), block)
        return to_peer(up_part.at[rows], up_recv.at[step - 1], up_ssem.at[step - 1], up_rsem.at[step - 1], step)

    def down_copy(step):
        return to_peer(down_send, down_all.at[sub], down_ssem.at[step - 1], down_rsem.at[step - 1], step)

    ways = (1, n_sub - 1)

    def mid_copy(c):
        return to_peer(pn_part.at[c, peer(2)], pn_mid.at[c], mid_sem.at[0, c], mid_sem.at[1, c], ways[c])

    def pn_copy(way, c):
        return to_peer(
            pn_part.at[c, peer(ways[way])], pn_recv.at[way, c], pn_ssem.at[way, c], pn_rsem.at[way, c], ways[way]
        )

    sides = (1, -1)

    def p_copy(i):
        if i < 2:
            source, there, device = mine, near_parent(-sides[i], core), on_chip(sides[i], core)
        elif i == 2:
            source, there, device = mine, near_parent(-2 * toward, core), on_chip(2 * toward, other)
        elif i == 3:
            source, there, device = mine, mine, sibling
        else:
            source = there = near_parent(-sides[i - 4], core)
            device = sibling
        return remote(window(source), window(there), p_ssem.at[i], p_rsem.at[i], device)

    far_sides = tuple(d for k in range(FAR_CHIPS, 0, -1) for d in (k, -k))

    def fx_copy():
        return remote(fx_send, fx_recv, fx_sem.at[0], fx_sem.at[1], sibling)

    def far_copy(i):
        return remote(far_send.at[i], far_recv.at[i], far_ssem.at[i], far_rsem.at[i], on_chip(far_sides[i], core))

    def ff_copy():
        return remote(far_recv, far_other, ff_sem.at[0], ff_sem.at[1], sibling)

    def ex_copy(i):
        return remote(ex_send.at[i], ex_recv.at[i], ex_sem.at[0, i], ex_sem.at[1, i], sibling)

    def qn_copy(i, c):
        device = (on_chip(toward, core), on_chip(-toward, core), on_chip(toward, other))[i]
        return remote(q_send.at[i, c], q_recv.at[i, c], qn_ssem.at[i, c], qn_rsem.at[i, c], device)

    steps = range(1, n_sub)
    far_first = sorted(steps, key=lambda step: -min(step, n_sub - step))
    for step in far_first:
        c_copy(step).start()
    for step in far_first:
        up_copy(step).start()
    for i in (2, 0, 1, 3):
        p_copy(i).start()
    for c in range(clusters):
        for step in far_first:
            q_copy(step, c).start()

    lax.fori_loop(0, n_keys, find, 0)
    lax.fori_loop(0, empty, find_last, 0)

    for step in steps:
        c_copy(step).wait()

    def gather_offset(w, carry):
        total = jnp.zeros((rank, 2 * rank), F32)
        for s in range(n_sub):
            here = coup_all[s, rank : rank + 1].astype(F32) == w.astype(F32)
            total = total + jnp.where(here, coup_all[s, :rank].astype(F32), 0.0)
        hi, lo = split(total + jnp.concatenate([total[:, rank:], total[:, :rank]], axis=1))
        cw_hi[w] = hi
        cw_lo[w] = lo
        return carry

    lax.fori_loop(0, FAR_SPAN, gather_offset, 0)

    for step in steps:
        up_copy(step).wait()
    up = up_part[pl.ds(pl.multiple_of(sub * block, block), block)]
    for step in steps:
        up = up + up_recv[step - 1]
    first = lane_half(up.shape)
    qg_hi, qg_lo = split(up[:, 64:])
    qg3 = jnp.concatenate([qg_hi, qg_lo, qg_hi], axis=1)

    def far_term(w):
        return mm(qg3, jnp.concatenate([cw_hi[w], cw_hi[w], cw_lo[w]], axis=0))

    for e in range(-FAR_CHIPS, FAR_CHIPS + 1):
        fx_send[e + FAR_CHIPS] = far_term(far_parent(e, other))
    fx_copy().start()
    far_own = [far_term(far_parent(e, core)) for e in range(-FAR_CHIPS, FAR_CHIPS + 1)]
    far_recv[2 * FAR_CHIPS] = up
    fx_copy().wait()

    def far_tile(e):
        return jnp.where(first, up, far_own[e + FAR_CHIPS] + fx_recv[e + FAR_CHIPS])

    for i, e in enumerate(far_sides):
        far_send[i] = far_tile(e)
        far_copy(i).start()
    own_tile = far_tile(0)

    for i in range(2):
        p_copy(i).wait()
        p_copy(4 + i).start()

    for c in range(clusters):
        tile_copy(c).wait()
    for i in range(2, 6):
        p_copy(i).wait()

    def near_products(c):
        def front(k, carry):
            a = table[at_block + c * slots + 2 * k]
            b = table[at_block + c * slots + 2 * k + 1]
            source = jnp.concatenate([p_win[a], p_win[b]], axis=1)
            pair = jnp.concatenate([tiles[c, 2 * k], tiles[c, 2 * k + 1]], axis=1)
            out = mm_nt(source, pair)
            for s in range(n_sub):
                pn_part[c, s] += out[:, s * quarter : (s + 1) * quarter]
            return carry

        pn_part[c] = jnp.zeros_like(pn_part[c])
        lax.fori_loop(0, slots // 2, front, 0, unroll=slots // 2)

    for c in range(clusters):
        near_products(c)
        mid_copy(c).start()
        pn_copy(1 - c, c).start()

    for c in range(clusters):
        for step in steps:
            q_copy(step, c).wait()
        q_rows = jnp.concatenate([q_all[s, c] for s in range(n_sub)], axis=1)

        def back(k, carry, c=c, q_rows=q_rows):
            j = c * slots + 2 * k
            pair = jnp.concatenate([tiles[c, 2 * k], tiles[c, 2 * k + 1]], axis=1)
            out = mm(q_rows, pair)
            chain[j] = out[:, :quarter] + chain[table[j]]
            chain[j + 1] = out[:, quarter:] + chain[table[j + 1]]
            return carry

        lax.fori_loop(0, slots // 2, back, 0, unroll=slots // 2)

    def back_to(parent, c):
        return chain[table[at_last + clusters * parent + c]]

    for c in range(clusters):
        q_send[2, c] = back_to(near_parent(2 * toward, other), c)
        qn_copy(2, c).start()
    for i, e in ((0, -toward), (2, toward), (1, 0)):
        for c in range(clusters):
            ex_send[i, c] = back_to(near_parent(e, other), c)
        ex_copy(i).start()
    ex_copy(0).wait()
    for c in range(clusters):
        q_send[0, c] = back_to(near_parent(toward, core), c) + ex_recv[0, c]
        qn_copy(0, c).start()

    ex_copy(2).wait()
    for c in range(clusters):
        q_send[1, c] = back_to(near_parent(-toward, core), c) + ex_recv[2, c]

    def far_lhs(x):
        hi, lo = split(jnp.where(first, x, 0.0))
        return jnp.concatenate([hi, lo, hi], axis=1)

    def far_rhs(w):
        return jnp.concatenate([cw_hi[w], cw_hi[w], cw_lo[w]], axis=1)

    for i in range(len(far_sides)):
        far_copy(i).wait()
    ff_copy().start()
    ph = mm_nt(far_lhs(own_tile), far_rhs(far_parent(0, core)))
    total = own_tile
    for i, e in enumerate(far_sides):
        got = far_recv[i]
        ph = ph + mm_nt(far_lhs(got), far_rhs(far_parent(-e, core)))
        total = total + got
    ff_copy().wait()
    for i, e in enumerate(far_sides + (0,)):
        ph = ph + mm_nt(far_lhs(far_other[i]), far_rhs(far_parent(-e, other)))

    down_send[...] = jnp.where(first, jnp.concatenate([ph, ph], axis=1), total)
    for step in far_first:
        down_copy(step).start()
    for c in range(clusters):
        qn_copy(2, c).wait()
        q_send[1, c] += q_recv[2, c]
        qn_copy(1, c).start()
    for c in range(clusters):
        mid_copy(c).wait()
        pn_part[c, peer(ways[c])] += pn_mid[c]
        pn_copy(c, c).start()
    down_all[sub] = down_send[...]
    for step in steps:
        down_copy(step).wait()
    coeff = jnp.concatenate([down_all[s] for s in range(n_sub)], axis=0)
    coeff_hi, coeff_lo = split(coeff)
    coeff3 = jnp.concatenate([coeff_hi, coeff_lo, coeff_hi], axis=1)
    far_hi, far_lo = diagonal(row_hi, col_hi), diagonal(row_lo, col_lo)
    far_field = mm(coeff3, jnp.concatenate([far_hi, far_hi, far_lo], axis=0))

    ex_copy(1).wait()
    for c in range(clusters):
        half = 0.5 * mass_ref[c : c + 1]
        t_ref[c] = half * p_ref[c].astype(F32) + far_field[:, c * quarter : (c + 1) * quarter] + pn_part[c, sub]
        u = half * q_all[sub, c].astype(F32) + far_field[:, (clusters + c) * quarter : (clusters + c + 1) * quarter]
        u_ref[c] = u + (back_to(mine, c) + ex_recv[1, c])

    for c in range(clusters):
        for way in range(2):
            pn_copy(way, c).wait()
        t_ref[c] = t_ref[c] + (pn_recv[0, c] + pn_recv[1, c])
    for c in range(clusters):
        for i in range(2):
            qn_copy(i, c).wait()
        u_ref[c] = u_ref[c] + (q_recv[0, c] + q_recv[1, c])

    outs = [
        pltpu.make_async_copy(src, dst, out_sem.at[i]) for i, (src, dst) in enumerate(((t_ref, t_hbm), (u_ref, u_hbm)))
    ]
    for out in outs:
        out.start()

    def by_rhs(x):
        return jnp.sum(x.T, axis=0, keepdims=True)

    half_rhs = rhs // 2
    tt = by_rhs(t_ref[0] * t_ref[0] + t_ref[1] * t_ref[1])
    uu = by_rhs(u_ref[0] * u_ref[0] + u_ref[1] * u_ref[1])
    tu = by_rhs(t_ref[0] * u_ref[0] + t_ref[1] * u_ref[1])
    halves = [x[:, k * half_rhs : (k + 1) * half_rhs] for x in (tt, uu, tu) for k in range(2)]
    sums = jnp.concatenate(halves + [jnp.zeros((2, half_rhs), F32)], axis=0)
    for g, (size, place, device) in enumerate(groups):
        ar[g, place] = sums

        def ar_copy(step, g=g, size=size, place=place, device=device):
            return pltpu.make_async_remote_copy(
                src_ref=ar.at[g, place],
                dst_ref=ar.at[g, place],
                send_sem=ar_ssem.at[g, step - 1],
                recv_sem=ar_rsem.at[g, step - 1],
                device_id=device(lax.rem(place + step, size)),
                device_id_type=MESH,
            )

        for step in range(1, size):
            ar_copy(step).start()
        for step in range(1, size):
            ar_copy(step).wait()
        sums = ar[g, 0]
        for i in range(1, size):
            sums = sums + ar[g, i]

    rho = 1.0 / jnp.sqrt(sums[0:2] + 1e-06)
    xi = 1.0 / jnp.sqrt(sums[2:4] + 1e-06)
    delta = sums[4:6] * (rho * xi)
    scale_ref[...] = jnp.concatenate([rho, xi, delta, jnp.zeros((2, half_rhs), F32)], axis=0)
    for out in outs:
        out.wait()


def scale_kernel(scale_ref, t_ref, u_ref, v_ref, w_ref, delta_ref):
    _, rhs, quarter = t_ref.shape
    half_rhs = rhs // 2
    for k, (src, dst) in enumerate(((t_ref, v_ref), (u_ref, w_ref))):
        for h in range(2):
            rows = slice(h * half_rhs, (h + 1) * half_rhs)
            factor = scale_ref[2 * k + h : 2 * k + h + 1]
            dst[0, rows] = src[0, rows] * jnp.broadcast_to(factor, (quarter, half_rhs)).T
    delta_ref[...] = jnp.concatenate([scale_ref[4:5], scale_ref[5:6]], axis=1)


def on_device(n_y, p_dir, q_dir, mass, tiles, near_ids, near_count, col, row, colt, rowt, coup, far_ids):
    clusters, rhs, quarter = p_dir.shape
    slots = tiles.shape[1]
    rank = col.shape[1]
    n_clu, n_sub = lax.axis_size("clu"), lax.axis_size("sub")
    block = rhs // n_sub
    n_keys = clusters * slots
    peers = n_sub - 1
    sides = 2 * FAR_CHIPS
    most = max(CORES * n_sub, n_y, n_clu // (n_y * CORES))
    vmem = pl.BlockSpec(memory_space=pltpu.VMEM)
    smem = pl.BlockSpec(memory_space=pltpu.SMEM)
    hbm = pl.BlockSpec(memory_space=pltpu.HBM)
    dma = pltpu.SemaphoreType.DMA
    whole = (clusters, rhs, quarter)
    t, u, scale = pl.pallas_call(
        functools.partial(kernel, (n_clu, n_sub, n_y)),
        out_shape=(
            jax.ShapeDtypeStruct(whole, F32),
            jax.ShapeDtypeStruct(whole, F32),
            jax.ShapeDtypeStruct((8, rhs // 2), F32),
        ),
        in_specs=[smem] * 3 + [hbm] * 9,
        out_specs=(hbm, hbm, vmem),
        scratch_shapes=[
            pltpu.SMEM((2 * n_keys + clusters * NEAR_SPAN,), jnp.int32),
            pltpu.VMEM(whole, F32),
            pltpu.VMEM(whole, F32),
            pltpu.VMEM(mass.shape, F32),
            pltpu.VMEM(col.shape, BF16),
            pltpu.VMEM(col.shape, BF16),
            pltpu.VMEM(colt.shape, BF16),
            pltpu.VMEM(colt.shape, BF16),
            pltpu.VMEM(coup.shape, BF16),
            pltpu.VMEM(tiles.shape, BF16),
            pltpu.VMEM((n_sub, *whole), BF16),
            pltpu.VMEM((n_sub, rank + 16, 2 * rank), BF16),
            pltpu.VMEM((clusters * NEAR_SPAN + 1, rhs, quarter), BF16),
            pltpu.VMEM((rhs, 2 * rank), F32),
            pltpu.VMEM((peers, block, 2 * rank), F32),
            pltpu.VMEM((FAR_SPAN, rank, 2 * rank), BF16),
            pltpu.VMEM((FAR_SPAN, rank, 2 * rank), BF16),
            pltpu.VMEM((sides + 1, block, 2 * rank), F32),
            pltpu.VMEM((sides + 1, block, 2 * rank), F32),
            pltpu.VMEM((sides, block, 2 * rank), F32),
            pltpu.VMEM((sides + 1, block, 2 * rank), F32),
            pltpu.VMEM((sides + 1, block, 2 * rank), F32),
            pltpu.VMEM((n_keys + 1, rhs, quarter), F32),
            pltpu.VMEM((3, *whole), F32),
            pltpu.VMEM((3, *whole), F32),
            pltpu.VMEM((3, *whole), F32),
            pltpu.VMEM((3, *whole), F32),
            pltpu.VMEM((clusters, n_sub, rhs, quarter), F32),
            pltpu.VMEM(whole, F32),
            pltpu.VMEM((2, *whole), F32),
            pltpu.VMEM((block, 2 * rank), F32),
            pltpu.VMEM((n_sub, block, 2 * rank), F32),
            pltpu.VMEM((3, most, 8, rhs // 2), F32),
            dma((2,)),
            dma((8,)),
            dma((clusters,)),
            dma((peers, clusters)),
            dma((peers, clusters)),
            dma((peers,)),
            dma((peers,)),
            dma((6,)),
            dma((6,)),
            dma((peers,)),
            dma((peers,)),
            dma((2,)),
            dma((sides,)),
            dma((sides,)),
            dma((2,)),
            dma((2, 3)),
            dma((3, clusters)),
            dma((3, clusters)),
            dma((2, clusters)),
            dma((2, clusters)),
            dma((2, clusters)),
            dma((peers,)),
            dma((peers,)),
            dma((3, most)),
            dma((3, most)),
        ],
        compiler_params=pltpu.CompilerParams(
            collective_id=0, has_side_effects=True, vmem_limit_bytes=VMEM_BYTES
        ),
    )(near_ids, near_count, far_ids, p_dir, q_dir, mass, col, row, colt, rowt, coup, tiles)
    one = pl.BlockSpec((1, rhs, quarter), lambda c: (c, 0, 0))
    v, w, delta = pl.pallas_call(
        scale_kernel,
        grid=(clusters,),
        out_shape=(
            jax.ShapeDtypeStruct(whole, F32),
            jax.ShapeDtypeStruct(whole, F32),
            jax.ShapeDtypeStruct((1, rhs), F32),
        ),
        in_specs=[pl.BlockSpec((8, rhs // 2), lambda c: (0, 0)), one, one],
        out_specs=(one, one, pl.BlockSpec((1, rhs), lambda c: (0, 0))),
        compiler_params=pltpu.CompilerParams(vmem_limit_bytes=VMEM_BYTES),
    )(scale, t, u)
    return v, w, delta.reshape(rhs)


def build(mesh, n_y):
    return jax.shard_map(
        functools.partial(on_device, n_y),
        mesh=mesh,
        in_specs=(
            P("clu", None, "sub"),
            P("clu", None, "sub"),
            P("clu", "sub"),
            P("clu", None, None, "sub"),
            P("clu", None),
            P("clu"),
            P("clu", None, "sub"),
            P("clu", None, "sub"),
            P("clu", None, None),
            P("clu", None, None),
            P("clu", "sub", None, None),
            P("clu", "sub"),
        ),
        out_specs=(P("clu", None, "sub"), P("clu", None, "sub"), P()),
        check_vma=False,
    )


def solution(mesh):
    return build(mesh, CHIPS_Y)
```
